512 devices in a mesh: seq: 64 (over z, y), head: 8 (over x, core).
Axes of the slice: x: 4, y: 4, z: 16, core: 2. Of those that a mesh axis runs over, the one named last changes fastest.
Arguments:
- hidden_in: bfloat16 [4, 16384], P(None, 'seq'), may hold values from -12 to 12
- norm_gain: float32 [16384], P('seq'), may hold values from 0.25 to 1.75
- qkv_codes: int32 [16384, 4608], P('seq', 'head'), may hold values from 0 to 255
- qkv_scale: float32 [18432], P('head'), may hold values from 0.00390625 to 0.015625
- out_codes: int32 [16384, 4096], P('seq', 'head'), may hold values from 0 to 255
- out_scale: float32 [16384], P('seq'), may hold values from 0.0078125 to 0.03125
- cache_keys: bfloat16 [4, 65536, 8, 128], P(None, 'seq', 'head'), may hold values from -200 to 200
- cache_values: bfloat16 [4, 65536, 8, 128], P(None, 'seq', 'head'), may hold values from -6 to 6
- lengths: int32 [4], replicated, may hold values from 32768 to 65536, as said below
Outputs:
- hidden_out: bfloat16 [4, 16384], P(None, 'seq')
The draws below stay inside these ranges and needn't reach their ends.
Inputs may be any that keep to these rules, and one draw needn't show every extreme that they name: `lengths`: some sequence uses all 65536 cached positions in every draw.
All inputs are finite; a program needn't handle non-finite values.
Results may differ from the reference program's by a relative error of at most 0.02.
The reference program's roundings to bfloat16 on the way (of `w_qkv`, `w_out`, `normed`, `queries`, `weights` and `attended`) count: a program that leaves them out, or rounds other values in their place, can miss the bound.
Values sent between devices are 32-bit elements; how exact they have to be, the bound alone decides.
No kernel may reach another device: no remote copies, remote signals or barrier semaphores. Data moves between devices by JAX's collectives and lax.ppermute only.
A program may use at most 64 MiB of HBM per device.

```python
import math
import jax
import jax.numpy as jnp
import numpy as np
from jax import lax

D = 16384
HEADS = 128
KV_HEADS = 8
HEAD_DIM = 128
TILE = 128
DECODE_STEPS = 2
BATCH = 4
CACHE_DEV = 1024
CACHE_LEN = 65536


def draw_hidden_in(key, part):
    places = jnp.arange(D, dtype=jnp.float32) / D
    ramp_scale = 0.6 + 1.2 * places
    values = jax.random.truncated_normal(key, -6.0, 6.0, (BATCH, D), jnp.float32)
    return (values * ramp_scale[None, :]).astype(jnp.bfloat16)


def draw_cache_keys(key, part):
    full_shape = (BATCH, CACHE_LEN, KV_HEADS, HEAD_DIM)
    values = 2.5 * jax.random.truncated_normal(key, -6.0, 6.0, full_shape, jnp.float32)
    return values.astype(jnp.bfloat16)


def draw_lengths(key, part):
    base_draw = jax.random.randint(jax.random.fold_in(key, 31), (BATCH,), CACHE_LEN // 2, CACHE_LEN)
    chosen_row = jax.random.randint(jax.random.fold_in(key, 32), (), 0, BATCH)
    return jnp.where(jnp.arange(BATCH) == chosen_row, CACHE_LEN, base_draw).astype(jnp.int32)


def with_ends(result, rng, smallest, largest):
    place = [jax.random.randint(jax.random.fold_in(rng, axis), (), 0, length) for axis, length in enumerate(result.shape)]
    widest = result.shape.index(max(result.shape))
    beside = place[:widest] + [(place[widest] + 1) % result.shape[widest]] + place[widest + 1:]
    return result.at[tuple(place)].set(smallest).at[tuple(beside)].set(largest)


def block_levels(key, shape, cuts, least, high):
    gain, own = 1.0, jax.random.fold_in(key, 6)
    for position, blocks in cuts:
        draws = jnp.exp(jax.random.uniform(jax.random.fold_in(own, position), (blocks,), jnp.float32, least / len(cuts), high / len(cuts)))
        gain = gain * jnp.repeat(draws, shape[position] // blocks).reshape([-1 if axis == position else 1 for axis in range(len(shape))])
    return gain


def centred(stream_key, extent, width, bound, shards=(), kind=jnp.bfloat16):
    values = jax.random.normal(stream_key, extent, jnp.float32) * width
    if len(shards) > 0:
        values = block_levels(stream_key, extent, shards, -0.22, 0.18) * values
    return jnp.clip(values, min=-bound, max=bound).astype(kind)


def setup_inputs(seed: int = 0) -> dict:
    keys = jax.random.split(jax.random.key(seed), 10)
    return {
        "hidden_in": draw_hidden_in(jax.random.fold_in(keys[9], 71), 0),
        "norm_gain": jnp.clip(1.0 + 0.15 * jax.random.normal(keys[1], (D,), jnp.float32), 0.25, 1.75),
        "qkv_codes": with_ends(jax.random.randint(keys[2], (D, KV_HEADS * (HEADS // KV_HEADS + 2) * HEAD_DIM // 4), 0, 256), jax.random.fold_in(keys[2], 1), 0, 255).astype(jnp.int32),
        "qkv_scale": jnp.clip(jnp.exp(math.log(0.015625) - 1.3862944 * jax.random.uniform(keys[3], (KV_HEADS * (HEADS // KV_HEADS + 2) * HEAD_DIM,), jnp.float32) ** block_levels(keys[3], (KV_HEADS * (HEADS // KV_HEADS + 2) * HEAD_DIM,), ((0, 8),), -0.2, 0.2)), 0.00390625, 0.015625),
        "out_codes": with_ends(jax.random.randint(keys[4], (D, HEADS * HEAD_DIM // 4), 0, 256), jax.random.fold_in(keys[4], 1), 0, 255).astype(jnp.int32),
        "out_scale": jnp.clip(jnp.exp(math.log(0.03125) - 1.3862944 * jax.random.uniform(keys[5], (D,), jnp.float32) ** block_levels(keys[5], (D,), ((0, 64),), -0.2, 0.2)), 0.0078125, 0.03125),
        "cache_keys": draw_cache_keys(jax.random.fold_in(keys[9], 71), 0),
        "cache_values": centred(keys[7], (BATCH, CACHE_LEN, KV_HEADS, HEAD_DIM), 1.0, 6.0, ((1, 64), (2, 8))),
        "lengths": draw_lengths(jax.random.fold_in(keys[9], 71), 0),
    }


code_norm = 147.8
epsilon = 1e-05
rope_base = 500000.0

def decode_codes(code_words):
    num_rows = code_words.shape[0]
    tile_bytes = TILE // 4
    byte_tiles = code_words.reshape(num_rows, -1, tile_bytes)
    byte_first = jnp.repeat(byte_tiles, 4, axis=2)
    byte_second = jnp.repeat(jnp.roll(byte_tiles, -1, axis=2), 4, axis=2)
    byte_third = jnp.repeat(jnp.roll(byte_tiles, -2, axis=2), 4, axis=2)
    window = byte_first * 65536 + byte_second * 256 + byte_third
    divisor = jnp.asarray(np.array([256, 64, 16, 4])[np.arange(TILE) % 4], dtype=jnp.int32)
    trellis_state = window // divisor % 65536
    low_product = trellis_state * 25297 + 13946
    low_half = low_product % 65536
    high_half = (trellis_state * 519 + 1169 + low_product // 65536) % 65536
    byte_total = low_half % 256 + low_half // 256 + high_half % 256 + high_half // 256
    return ((byte_total - 510).astype(jnp.float32) / code_norm).reshape(num_rows, -1)

def rope_tables(positions):
    half_dim = HEAD_DIM // 2
    freqs = jnp.exp(-(jnp.arange(half_dim, dtype=jnp.float32) * (2.0 / HEAD_DIM)) * math.log(rope_base))
    angles = positions.astype(jnp.float32)[:, None] * freqs[None, :]
    return (jnp.cos(angles), jnp.sin(angles))

def rotate(values, cosine_table, sine_table):
    half_dim = values.shape[-1] // 2
    first_half = values[..., :half_dim]
    second = values[..., half_dim:]
    return jnp.concatenate([first_half * cosine_table - second * sine_table, second * cosine_table + first_half * sine_table], axis=-1)

def finish(top_max, denominator, numerator, queries, new_keys, new_values):
    score_scale = HEAD_DIM ** (-0.5)
    query_float = queries.astype(jnp.float32)
    new_scores = [lax.optimization_barrier(jnp.sum(query_float * new_key.astype(jnp.float32)[:, :, None, :], axis=-1)) * score_scale for new_key in new_keys]
    peak_score = top_max
    for new_score in new_scores:
        peak_score = jnp.maximum(peak_score, new_score)
    factor = jnp.exp(top_max - peak_score)
    denominator = denominator * factor
    numerator = numerator * factor[..., None]
    for new_score, new_value in zip(new_scores, new_values):
        weight_new = jnp.exp(new_score - peak_score)
        denominator = denominator + weight_new
        numerator = numerator + weight_new[..., None] * new_value.astype(jnp.float32)[:, :, None, :]
    attended = numerator / denominator[..., None]
    return attended.astype(jnp.bfloat16).reshape(attended.shape[0], -1)

def cache_part(queries, cache_keys, cache_values, lengths):
    score_scale = HEAD_DIM ** (-0.5)
    blocks = CACHE_LEN // CACHE_DEV
    live_mask = (jnp.arange(CACHE_LEN, dtype=jnp.int32)[None, :] < lengths[:, None]).reshape(BATCH, 1, blocks, CACHE_DEV)

    def one_head(operands):
        head_query, head_keys, head_values = operands
        scores = jnp.einsum('brd,bld->brl', head_query.astype(jnp.float32), head_keys.astype(jnp.float32)) * score_scale
        scores = scores.reshape(BATCH, -1, blocks, CACHE_DEV)
        block_max = lax.optimization_barrier(jnp.max(jnp.where(live_mask, scores, -1e+30), axis=3))
        weights = jnp.where(live_mask, jnp.exp(scores - block_max[..., None]), 0.0)
        block_sum = lax.optimization_barrier(jnp.sum(weights, axis=3))
        rounded = lax.optimization_barrier(weights.astype(jnp.bfloat16)).astype(jnp.float32)
        block_values = head_values.astype(jnp.float32).reshape(BATCH, blocks, CACHE_DEV, HEAD_DIM)
        block_acc = jnp.einsum('brnc,bncd->brnd', rounded, block_values)
        top_max = lax.optimization_barrier(jnp.max(block_max, axis=2))
        factor = jnp.exp(block_max - top_max[..., None])
        return (top_max, lax.optimization_barrier(jnp.sum(block_sum * factor, axis=2)), lax.optimization_barrier(jnp.sum(block_acc * factor[..., None], axis=2)))
    stacked = lax.map(one_head, (jnp.moveaxis(queries, 1, 0), jnp.moveaxis(cache_keys, 2, 0), jnp.moveaxis(cache_values, 2, 0)))
    return tuple((jnp.moveaxis(member, 0, 1) for member in stacked))

def reference(hidden_in, norm_gain, qkv_codes, qkv_scale, out_codes, out_scale, cache_keys, cache_values, lengths):
    row_block = math.gcd(D, 512)

    def decode_qkv(code_block):
        return (decode_codes(code_block) * qkv_scale[None, :]).astype(jnp.bfloat16)

    def decode_out(operands):
        code_block, scale_block = operands
        return (decode_codes(code_block) * scale_block[:, None]).astype(jnp.bfloat16)
    w_qkv = lax.map(decode_qkv, qkv_codes.reshape(D // row_block, row_block, -1)).reshape(D, -1)
    w_out = lax.map(decode_out, (out_codes.reshape(D // row_block, row_block, -1), out_scale.reshape(D // row_block, row_block))).reshape(D, -1)
    groups = HEADS // KV_HEADS
    hidden = hidden_in
    new_keys = []
    new_values = []
    for decode_step in range(DECODE_STEPS):
        positions = lengths + decode_step
        squares = lax.optimization_barrier(jnp.sum(jnp.square(hidden.astype(jnp.float32)), axis=1))
        normed = (hidden.astype(jnp.float32) * norm_gain[None, :]).astype(jnp.bfloat16)
        projected = jnp.dot(normed, w_qkv, preferred_element_type=jnp.float32)
        projected = projected * lax.rsqrt(squares / D + epsilon)[:, None]
        grouped = projected.reshape(BATCH, KV_HEADS, groups + 2, HEAD_DIM)
        cosine_table, sine_table = rope_tables(positions)
        queries = rotate(grouped[:, :, :groups], cosine_table[:, None, None, :], sine_table[:, None, None, :]).astype(jnp.bfloat16)
        new_keys.append(rotate(grouped[:, :, groups], cosine_table[:, None, :], sine_table[:, None, :]).astype(jnp.bfloat16))
        new_values.append(grouped[:, :, groups + 1].astype(jnp.bfloat16))
        top_max, denominator, numerator = cache_part(queries, cache_keys, cache_values, lengths)
        attended = finish(top_max, denominator, numerator, queries, new_keys, new_values)
        update = lax.dot_general(attended, w_out, (((1,), (1,)), ((), ())), preferred_element_type=jnp.float32)
        hidden = (hidden.astype(jnp.float32) + update).astype(jnp.bfloat16)
    return hidden
```

```python
import functools
import math

import jax
import jax.numpy as jnp
from jax import lax
from jax.experimental import pallas as pl
from jax.experimental.pallas import tpu as pltpu
from jax.sharding import Mesh
from jax.sharding import PartitionSpec as P

HEAD_DIM = 128
GROUPS = 16
DECODE_STEPS = 2
NEAR = ("z_low", "y")
FAR = "z_high"
SEQ = (FAR, *NEAR)

CODE_NORM = 147.8
EPSILON = 1e-05
ROPE_BASE = 500000.0
SCORE_SCALE = HEAD_DIM ** (-0.5)

GROUP_ROW = (0, 512, 1152, 1664)
GROUP_PLACE = (0, 2, 1, 3)
TAIL_ROW = (1024, 2176)

f32 = jnp.float32
bf16 = jnp.bfloat16
NT = (((1,), (1,)), ((), ()))


def iota(shape, axis):
    return lax.broadcasted_iota(jnp.int32, shape, axis)


def call(kernel, outs, name):
    return pl.pallas_call(
        kernel,
        out_shape=outs,
        name=name,
        compiler_params=pltpu.CompilerParams(vmem_limit_bytes=48 * 1024 * 1024),
    )


def shape_of(shape, dtype=f32):
    return jax.ShapeDtypeStruct(shape, dtype)


def byte_sum(state):
    x = state * 34038481 + 76625530
    pairs = (x & 0x00FF00FF) + ((x >> 8) & 0x00FF00FF)
    total = (pairs + (pairs >> 16)) & 0x7FF
    return (total - 510).astype(f32)


def interleave():
    row = iota((512, 512), 0)
    column = iota((512, 512), 1)
    return (column == 4 * (row & 127) + (row >> 7)).astype(f32).astype(bf16)


def by_sequence():
    row = iota((64, 64), 0)
    column = iota((64, 64), 1)
    return (column == 4 * (row & 15) + (row >> 4)).astype(f32).astype(bf16)


def exact_product(x, ones):
    rows = x.shape[0]
    high = x.astype(bf16).astype(f32)
    rest = x - high
    middle = rest.astype(bf16).astype(f32)
    low = rest - middle
    parts = jnp.concatenate([high, middle, low, jnp.zeros_like(low)], axis=0).astype(bf16)
    product = jnp.dot(parts, ones, preferred_element_type=f32)
    return product[:rows] + product[rows : 2 * rows] + product[2 * rows : 3 * rows]


def project(hidden, gain, weights, out_ref):
    squares = jnp.sum(hidden * hidden, axis=1, keepdims=True)
    normed = (hidden * gain).astype(bf16)
    y = lax.dot_general(normed, weights, NT, preferred_element_type=f32)
    half = y.shape[1] // 2
    first = iota((8, half), 0) < 4
    packed = jnp.where(first, y[:, :half], y[:, half:])
    spread = jnp.broadcast_to(squares, (8, 128))
    for j in range(out_ref.shape[0]):
        out_ref[j, :, :half] = packed
        out_ref[j, :, half:] = spread


def decode_qkv_kernel(hidden_ref, gain_ref, codes_ref, scale_ref, w_ref, hid_ref, out_ref):
    lane = iota((32, 128), 1)
    word = iota((32, 128), 0)
    for tile in range(18):
        codes = codes_ref[tile * 32 : tile * 32 + 32, :]
        window = (codes << 16) | (pltpu.roll(codes, 31, 0) << 8) | pltpu.roll(codes, 30, 0)
        scales = jnp.broadcast_to(scale_ref[tile : tile + 1, :], (32, 128)) * (1.0 / CODE_NORM)
        for r in range(4):
            column = jnp.sum(
                jnp.where(lane == 4 * word + r, scales, 0.0), axis=1, keepdims=True
            )
            values = byte_sum((window >> (8 - 2 * r)) & 0xFFFF) * column
            if tile < 16:
                at = GROUP_ROW[tile // 4] + r * 128 + (tile % 4) * 32
            else:
                at = TAIL_ROW[r // 2] + (r % 2) * 64 + (tile - 16) * 32
            w_ref[at : at + 32, :] = values.astype(bf16)
    hidden = hidden_ref[...].astype(f32)
    hidden = jnp.concatenate([hidden, hidden], axis=0)
    hid_ref[...] = hidden
    project(hidden, gain_ref[...], w_ref[...], out_ref)


def decode_out_kernel(codes_ref, scale_ref, w_ref):
    lane = iota((32, 128), 1)
    within = lane & 31
    for block in range(8):
        rows = slice(block * 32, block * 32 + 32)
        across = iota((32, 256), 1) == iota((32, 256), 0) + block * 32
        scale = jnp.broadcast_to(scale_ref[...], (32, 256)) * (1.0 / CODE_NORM)
        column = jnp.sum(jnp.where(across, scale, 0.0), axis=1, keepdims=True)
        for group in range(4):
            codes = codes_ref[rows, group * 128 : group * 128 + 128]
            second = jnp.where(within < 31, pltpu.roll(codes, 127, 1), pltpu.roll(codes, 31, 1))
            third = jnp.where(within < 30, pltpu.roll(codes, 126, 1), pltpu.roll(codes, 30, 1))
            window = (codes << 16) | (second << 8) | third
            for r in range(4):
                values = byte_sum((window >> (8 - 2 * r)) & 0xFFFF) * column
                at = group * 512 + r * 128
                w_ref[rows, at : at + 128] = values.astype(bf16)


def total_of(ref):
    total = ref[0]
    for j in range(1, ref.shape[0]):
        total = total + ref[j]
    return total


def pass_sum_kernel(in_ref, out_ref):
    total = total_of(in_ref)
    for j in range(out_ref.shape[0]):
        out_ref[j] = total


def store_partial(out_ref, m_row, l_row, acc):
    stats = jnp.concatenate([m_row, l_row], axis=1)
    stats = jnp.broadcast_to(stats, (8, 128))
    for j in range(out_ref.shape[0]):
        out_ref[j, :64, :] = acc
        out_ref[j, 64:, :] = stats


def merged(in_ref):
    count = in_ref.shape[0]
    stats = [in_ref[j, 64:65, :] for j in range(count)]
    top = functools.reduce(jnp.maximum, [s[:, :64] for s in stats])
    factors = [jnp.exp(s[:, :64] - top) for s in stats]
    sums = functools.reduce(lambda a, b: a + b, [s[:, 64:] * w for s, w in zip(stats, factors)])
    across = iota((64, 64), 0) == iota((64, 64), 1)

    def as_column(row):
        return jnp.sum(jnp.where(across, jnp.broadcast_to(row, (64, 64)), 0.0), axis=1, keepdims=True)

    acc = in_ref[0, :64, :] * as_column(factors[0])
    for j in range(1, count):
        acc = acc + in_ref[j, :64, :] * as_column(factors[j])
    return top, sums, acc, as_column


def pass_merge_kernel(in_ref, out_ref):
    top, sums, acc, _ = merged(in_ref)
    store_partial(out_ref, top, sums, acc)


def attend_kernel(features, limit_ref, in_ref, cos_ref, sin_ref, keys_ref, values_ref,
                  out_ref, q_ref, k_ref, v_ref):
    y = total_of(in_ref)
    rms = lax.rsqrt(y[:, 1152:] / features + EPSILON)
    y = y[:, :1152] * jnp.concatenate([rms] * 9, axis=1)
    heads = jnp.concatenate([y[:, :512], y[:, 512:1024]], axis=0)
    heads = exact_product(heads, interleave())
    row = iota((128, 512), 0)
    column = iota((128, 512), 1)
    where_to = ((row >> 5) & 1) * 128 + 4 * (row & 31) + (row >> 6) + 2 * (column >> 8)
    spread = ((column & 255) == where_to).astype(f32).astype(bf16)
    tail = exact_product(y[:, 1024:], spread)
    tail = tail[:, :256] + pltpu.roll(tail[:, 256:], 4, 0)
    cos = cos_ref[...]
    sin = sin_ref[...]
    key = tail[:, :128]
    key = key * cos + pltpu.roll(key, 64, 1) * sin
    k_ref[...] = key.astype(bf16).astype(f32)
    v_ref[...] = tail[:, 128:].astype(bf16).astype(f32)
    cos = jnp.concatenate([cos, cos], axis=0)
    sin = jnp.concatenate([sin, sin], axis=0)
    turned = []
    for tile in range(4):
        part = heads[:, tile * 128 : tile * 128 + 128]
        turned.append(part * cos + pltpu.roll(part, 64, 1) * sin)
    queries = jnp.concatenate(turned, axis=0).astype(bf16)
    queries = jnp.dot(by_sequence(), queries, preferred_element_type=f32)
    q_ref[...] = queries
    queries = queries.astype(bf16)
    length = keys_ref.shape[1]
    place = iota((16, length), 1)
    maxima, sums, accs = [], [], []
    for b in range(4):
        scores = lax.dot_general(
            queries[b * 16 : b * 16 + 16], keys_ref[b], NT, preferred_element_type=f32
        ) * SCORE_SCALE
        live = place < limit_ref[b]
        top = jnp.max(jnp.where(live, scores, -1e30), axis=1, keepdims=True)
        weights = jnp.where(live, jnp.exp(scores - top), 0.0)
        maxima.append(top)
        sums.append(jnp.sum(weights, axis=1, keepdims=True))
        accs.append(jnp.dot(weights.astype(bf16), values_ref[b], preferred_element_type=f32))
    across = iota((64, 64), 0) == iota((64, 64), 1)

    def as_row(columns):
        column = jnp.broadcast_to(jnp.concatenate(columns, axis=0), (64, 64))
        return jnp.sum(jnp.where(across, column, 0.0), axis=0, keepdims=True)

    store_partial(out_ref, as_row(maxima), as_row(sums), jnp.concatenate(accs, axis=0))


def finish_kernel(steps, in_ref, q_ref, w_ref, *refs):
    out_ref = refs[-1]
    top, sums, acc, as_column = merged(in_ref)
    top, denominator = as_column(top), as_column(sums)
    queries = q_ref[...]

    def by_head(ref):
        return jnp.concatenate(
            [jnp.broadcast_to(ref[b : b + 1, :], (16, 128)) for b in range(4)], axis=0
        )

    scores = [
        jnp.sum(queries * by_head(refs[2 * u]), axis=1, keepdims=True) * SCORE_SCALE
        for u in range(steps)
    ]
    peak = functools.reduce(jnp.maximum, scores, top)
    factor = jnp.exp(top - peak)
    denominator = denominator * factor
    numerator = acc * factor
    for u in range(steps):
        weight = jnp.exp(scores[u] - peak)
        denominator = denominator + weight
        numerator = numerator + weight * by_head(refs[2 * u + 1])
    attended = (numerator / denominator).astype(bf16)
    attended = lax.dot_general(
        by_sequence(), attended, (((0,), (0,)), ((), ())), preferred_element_type=f32
    )
    attended = jnp.concatenate([attended[t * 16 : t * 16 + 16] for t in range(4)], axis=1)
    attended = lax.dot_general(
        attended.astype(bf16), interleave(), NT, preferred_element_type=f32
    )
    place = iota((16, 512), 0) >> 2
    columns = jnp.concatenate(
        [jnp.where(place == GROUP_PLACE[g], attended, 0.0) for g in range(4)], axis=1
    ).astype(bf16)
    update = lax.dot_general(columns, w_ref[...], NT, preferred_element_type=f32)
    update = update[:8] + update[8:]
    update = update + pltpu.roll(update, 4, 0)
    packed = jnp.where(iota((8, 128), 0) < 4, update[:, :128], update[:, 128:])
    for j in range(out_ref.shape[0]):
        out_ref[j] = packed


def updated(in_ref, hid_ref):
    update = total_of(in_ref)
    turned = pltpu.roll(update, 4, 0)
    first = iota((8, 128), 0) < 4
    update = jnp.concatenate(
        [jnp.where(first, update, turned), jnp.where(first, turned, update)], axis=1
    )
    return (hid_ref[...] + update).astype(bf16)


def next_kernel(in_ref, hid_ref, gain_ref, w_ref, new_ref, out_ref):
    hidden = updated(in_ref, hid_ref).astype(f32)
    new_ref[...] = hidden
    project(hidden, gain_ref[...], w_ref[...], out_ref)


def last_kernel(in_ref, hid_ref, out_ref):
    out_ref[...] = updated(in_ref, hid_ref)[:4]


def exchange(value, axes):
    return lax.all_to_all(value, axes, split_axis=0, concat_axis=0, tiled=True)


def shards(features, hidden_in, norm_gain, qkv_codes, qkv_scale, out_codes, out_scale,
           cache_keys, cache_values, lengths):
    near = lax.axis_size(NEAR)
    far = lax.axis_size(FAR)
    heads = lax.axis_size("head")
    gain = norm_gain.reshape(1, -1)
    batch, block_len = cache_keys.shape[:2]
    keys = cache_keys.reshape(batch, block_len, HEAD_DIM)
    values = cache_values.reshape(batch, block_len, HEAD_DIM)
    limit = lengths - lax.axis_index(SEQ) * block_len

    half_dim = HEAD_DIM // 2
    freqs = jnp.exp(
        -(jnp.arange(half_dim, dtype=f32) * (2.0 / HEAD_DIM)) * math.log(ROPE_BASE)
    )
    steps = jnp.arange(DECODE_STEPS, dtype=jnp.int32)
    positions = lengths[None, :] + steps[:, None]
    angles = positions.astype(f32)[:, :, None] * freqs
    cosines, sines = jnp.cos(angles), jnp.sin(angles)
    cosines = jnp.tile(jnp.concatenate([cosines, cosines], axis=-1), (1, 2, 1))
    sines = jnp.tile(jnp.concatenate([-sines, sines], axis=-1), (1, 2, 1))

    w_qkv, hidden, partial = call(
        decode_qkv_kernel,
        (shape_of((2304, 256), bf16), shape_of((8, 256)), shape_of((near, 8, 1280))),
        "decode_qkv",
    )(hidden_in, gain, qkv_codes.T, qkv_scale.reshape(18, 128))
    w_out = call(decode_out_kernel, shape_of((256, 2048), bf16), "decode_out")(
        out_codes, out_scale.reshape(1, -1)
    )
    fresh = []
    for step in range(DECODE_STEPS):
        partial = exchange(partial, NEAR)
        partial = call(pass_sum_kernel, shape_of((far, 8, 1280)), "pass_sum")(partial)
        partial = exchange(partial, FAR)
        part, queries, new_key, new_value = pl.pallas_call(
            functools.partial(attend_kernel, features),
            out_shape=(
                shape_of((near, 72, 128)),
                shape_of((64, 128)),
                shape_of((8, 128)),
                shape_of((8, 128)),
            ),
            in_specs=[pl.BlockSpec(memory_space=pltpu.SMEM)]
            + [pl.BlockSpec(memory_space=pltpu.VMEM)] * 5,
            name="attend",
            compiler_params=pltpu.CompilerParams(vmem_limit_bytes=48 * 1024 * 1024),
        )(limit, partial, cosines[step], sines[step], keys, values)
        fresh += [new_key, new_value]
        part = exchange(part, NEAR)
        part = call(pass_merge_kernel, shape_of((far, 72, 128)), "pass_merge")(part)
        part = exchange(part, FAR)
        update = call(
            functools.partial(finish_kernel, step + 1), shape_of((heads, 8, 128)), "finish"
        )(part, queries, w_out, *fresh)
        update = exchange(update, "head")
        if step + 1 < DECODE_STEPS:
            hidden, partial = call(
                next_kernel, (shape_of((8, 256)), shape_of((near, 8, 1280))), "next_step"
            )(update, hidden, gain, w_qkv)
    return call(last_kernel, shape_of((4, 256), bf16), "last")(update, hidden)


def solution(mesh):
    seq, head = mesh.shape["seq"], mesh.shape["head"]
    far = seq // 8
    split = Mesh(mesh.devices.reshape(far, 2, 4, head), (*SEQ, "head"))
    placed = (
        P(None, SEQ),
        P(SEQ),
        P(SEQ, "head"),
        P("head"),
        P(SEQ, "head"),
        P(SEQ),
        P(None, SEQ, "head", None),
        P(None, SEQ, "head", None),
        P(),
    )

    def run(hidden_in, *others):
        features = hidden_in.shape[1]
        return jax.shard_map(
            functools.partial(shards, float(features)),
            mesh=split,
            in_specs=placed,
            out_specs=P(None, SEQ),
            check_vma=False,
        )(hidden_in, *others)

    return run
```

```python
import functools
import math

import jax
import jax.numpy as jnp
from jax import lax
from jax.experimental import pallas as pl
from jax.experimental.pallas import tpu as pltpu
from jax.sharding import Mesh
from jax.sharding import PartitionSpec as P

HEAD_DIM = 128
GROUPS = 16
DECODE_STEPS = 2
NEAR = ("z_low", "y")
FAR = "z_high"
SEQ = (FAR, *NEAR)

CODE_NORM = 147.8
EPSILON = 1e-05
ROPE_BASE = 500000.0
SCORE_SCALE = HEAD_DIM ** (-0.5)

f32 = jnp.float32
bf16 = jnp.bfloat16
NT = (((1,), (1,)), ((), ()))


def iota(shape, axis):
    return lax.broadcasted_iota(jnp.int32, shape, axis)


def call(kernel, outs, name, arrays, scalars=()):
    specs = [pl.BlockSpec(memory_space=pltpu.SMEM) for _ in scalars]
    specs += [pl.BlockSpec(memory_space=pltpu.VMEM) for _ in arrays]
    return pl.pallas_call(
        kernel,
        out_shape=outs,
        in_specs=specs,
        name=name,
        compiler_params=pltpu.CompilerParams(vmem_limit_bytes=32 * 1024 * 1024),
    )(*scalars, *arrays)


def shape_of(shape, dtype=f32):
    return jax.ShapeDtypeStruct(shape, dtype)


def byte_sum(state):
    x = state * 34038481 + 76625530
    pairs = (x & 0x00FF00FF) + ((x >> 8) & 0x00FF00FF)
    total = (pairs + (pairs >> 16)) & 0x7FF
    return (total - 510).astype(f32)


def interleave():
    row = iota((128, 128), 0)
    column = iota((128, 128), 1)
    return (column == 4 * (row & 31) + (row >> 5)).astype(f32).astype(bf16)


def by_sequence():
    row = iota((64, 64), 0)
    column = iota((64, 64), 1)
    return (column == 4 * (row & 15) + (row >> 4)).astype(f32).astype(bf16)


def by_place():
    row = iota((32, 32), 0)
    column = iota((32, 32), 1)
    source = 8 * (row & 3) + (row & 4) + (row >> 3)
    return (column == source).astype(f32).astype(bf16)


def exact_product(x, ones):
    rows = x.shape[0]
    high = x.astype(bf16).astype(f32)
    rest = x - high
    middle = rest.astype(bf16).astype(f32)
    low = rest - middle
    parts = jnp.concatenate([high, middle, low], axis=0).astype(bf16)
    product = jnp.dot(parts, ones, preferred_element_type=f32)
    return product[:rows] + product[rows : 2 * rows] + product[2 * rows :]


def tile_of(x, k):
    return x[:, k * 128 : k * 128 + 128]


def send_halves(out_ref, halves):
    copies = out_ref.shape[0] // 2
    for s in range(2):
        for j in range(copies):
            for k in range(5):
                out_ref[s * copies + j, :, k * 128 : k * 128 + 128] = halves[s][k]


def project(hidden, gain, weights, out_ref):
    squares = jnp.sum(hidden * hidden, axis=1, keepdims=True)
    normed = (hidden * gain).astype(bf16)
    y = lax.dot_general(normed, weights, NT, preferred_element_type=f32)
    first = iota((8, 128), 0) < 4
    spread = jnp.broadcast_to(squares, (8, 128))
    halves = []
    for s in range(2):
        tiles = [
            jnp.where(first, tile_of(y, 8 * s + 2 * i), tile_of(y, 8 * s + 2 * i + 1))
            for i in range(4)
        ]
        halves.append(tiles + [jnp.where(first, tile_of(y, 16 + s), spread)])
    send_halves(out_ref, halves)


def decode_qkv_kernel(hidden_ref, gain_ref, codes_ref, scale_ref, w_ref, hid_ref, out_ref):
    lane = iota((32, 128), 1)
    word = iota((32, 128), 0)
    for tile in range(18):
        codes = codes_ref[tile * 32 : tile * 32 + 32, :]
        window = (codes << 16) | (pltpu.roll(codes, 31, 0) << 8) | pltpu.roll(codes, 30, 0)
        scales = jnp.broadcast_to(scale_ref[tile : tile + 1, :], (32, 128)) * (1.0 / CODE_NORM)
        for r in range(4):
            column = jnp.sum(
                jnp.where(lane == 4 * word + r, scales, 0.0), axis=1, keepdims=True
            )
            values = byte_sum((window >> (8 - 2 * r)) & 0xFFFF) * column
            at = tile * 128 + r * 32
            w_ref[at : at + 32, :] = values.astype(bf16)
    hidden = hidden_ref[...].astype(f32)
    hidden = jnp.concatenate([hidden, hidden], axis=0)
    hid_ref[...] = hidden
    project(hidden, gain_ref[...], w_ref[...], out_ref)


def decode_out_kernel(info_ref, codes_ref, scale_ref, other_ref, w_ref):
    s = info_ref[5]
    lane = iota((32, 128), 1)
    within = lane & 31
    for block in range(16):
        own = block < 8
        rows = slice(block % 8 * 32, block % 8 * 32 + 32)
        across = iota((32, 256), 1) == iota((32, 256), 0) + block % 8 * 32
        scale = scale_ref[...] if own else other_ref[256:257, :]
        scale = jnp.broadcast_to(scale, (32, 256)) * (1.0 / CODE_NORM)
        column = jnp.sum(jnp.where(across, scale, 0.0), axis=1, keepdims=True)
        for group in range(2):
            if own:
                codes = jnp.where(
                    s == 0,
                    codes_ref[rows, group * 128 : group * 128 + 128],
                    codes_ref[rows, group * 128 + 256 : group * 128 + 384],
                )
            else:
                codes = other_ref[rows, group * 128 : group * 128 + 128].astype(jnp.int32)
            second = jnp.where(within < 31, pltpu.roll(codes, 127, 1), pltpu.roll(codes, 31, 1))
            third = jnp.where(within < 30, pltpu.roll(codes, 126, 1), pltpu.roll(codes, 30, 1))
            window = (codes << 16) | (second << 8) | third
            for r in range(4):
                values = byte_sum((window >> (8 - 2 * r)) & 0xFFFF) * column
                at = group * 512 + r * 128
                w_ref[block * 32 : block * 32 + 32, at : at + 128] = values.astype(bf16)


def total_of(ref):
    total = ref[0]
    for j in range(1, ref.shape[0]):
        total = total + ref[j]
    return total


def pass_sum_kernel(in_ref, out_ref):
    total = total_of(in_ref)
    for j in range(out_ref.shape[0]):
        out_ref[j] = total


def merged(in_ref):
    parts = range(in_ref.shape[0])
    stats = [in_ref[j, :, 512:] for j in parts]
    top = functools.reduce(jnp.maximum, stats)
    factors = [jnp.exp(x - top) for x in stats]
    sums = stats[0] * pltpu.roll(factors[0], 4, 1)
    for j in parts[1:]:
        sums = sums + stats[j] * pltpu.roll(factors[j], 4, 1)
    accs = []
    for b in range(4):
        at = slice(b * 128, b * 128 + 128)
        acc = in_ref[0, :, at] * factors[0][:, b : b + 1]
        for j in parts[1:]:
            acc = acc + in_ref[j, :, at] * factors[j][:, b : b + 1]
        accs.append(acc)
    return top, sums, accs


def pass_merge_kernel(in_ref, out_ref):
    top, sums, accs = merged(in_ref)
    lane = iota((8, 128), 1)
    stats = jnp.where(lane < 4, top, jnp.where(lane < 8, sums, 0.0))
    for j in range(out_ref.shape[0]):
        for b in range(4):
            out_ref[j, :, b * 128 : b * 128 + 128] = accs[b]
        out_ref[j, :, 512:] = stats


def attend_kernel(features, earlier, info_ref, in_ref, cos_ref, sin_ref, keys_ref, values_ref,
                  *refs):
    out_ref, k_ref, v_ref = refs[2 * earlier :]
    first = iota((8, 128), 0) < 4
    last = in_ref[0, :, 512:]
    squares = jnp.where(first, pltpu.roll(last, 4, 0), last)
    rms = lax.rsqrt(squares / features + EPSILON)
    tiles = [tile_of(in_ref[s], i) * rms for s in range(2) for i in range(4)]
    tiles += [in_ref[s, :, 512:] * rms for s in range(2)]
    x = exact_product(jnp.concatenate(tiles, axis=0), interleave())
    cos = jnp.concatenate([cos_ref[...]] * 9, axis=0)
    sin = jnp.concatenate([sin_ref[...]] * 9, axis=0)
    turned = x[:72] * cos + pltpu.roll(x[:72], 64, 1) * sin
    turned = turned.astype(bf16)
    new_key = turned[64:72].astype(f32)
    new_value = x[72:].astype(bf16).astype(f32)
    k_ref[...] = new_key
    v_ref[...] = new_value
    queries = jnp.dot(by_sequence(), turned[:64], preferred_element_type=f32)
    new_keys = [refs[2 * u][...] for u in range(earlier)] + [new_key]
    new_values = [refs[2 * u + 1][...] for u in range(earlier)] + [new_value]
    owner = info_ref[4] == 0
    length = keys_ref.shape[1]
    place = iota((16, length), 1)
    lane = iota((8, 128), 1)
    halves = [[], []]
    stats = [jnp.zeros((8, 128), f32)] * 2
    for b in range(4):
        query = queries[b * 16 : b * 16 + 16]
        scores = lax.dot_general(
            query.astype(bf16), keys_ref[b], NT, preferred_element_type=f32
        ) * SCORE_SCALE
        live = place < info_ref[b]
        top = jnp.max(jnp.where(live, scores, -1e30), axis=1, keepdims=True)
        weights = jnp.where(live, jnp.exp(scores - top), 0.0)
        total = jnp.sum(weights, axis=1, keepdims=True)
        acc = jnp.dot(weights.astype(bf16), values_ref[b], preferred_element_type=f32)
        fresh = [
            jnp.where(
                owner,
                jnp.sum(query * key[b : b + 1, :], axis=1, keepdims=True) * SCORE_SCALE,
                -1e30,
            )
            for key in new_keys
        ]
        peak = functools.reduce(jnp.maximum, fresh, top)
        factor = jnp.exp(top - peak)
        total = total * factor
        acc = acc * factor
        for score, value in zip(fresh, new_values):
            weight = jnp.where(owner, jnp.exp(score - peak), 0.0)
            total = total + weight
            acc = acc + weight * value[b : b + 1, :]
        for s in range(2):
            rows = slice(8 * s, 8 * s + 8)
            halves[s].append(acc[rows])
            stats[s] = jnp.where(lane == b, peak[rows], stats[s])
            stats[s] = jnp.where(lane == 4 + b, total[rows], stats[s])
    send_halves(out_ref, [halves[s] + [stats[s]] for s in range(2)])


def finish_kernel(info_ref, in_ref, w_ref, out_ref):
    _, sums, accs = merged(in_ref)
    attended = jnp.concatenate(
        [accs[b] / sums[:, 4 + b : 5 + b] for b in range(4)], axis=0
    ).astype(bf16)
    attended = jnp.dot(by_place(), attended, preferred_element_type=f32).astype(bf16)
    attended = lax.dot_general(attended, interleave(), NT, preferred_element_type=f32)
    block = iota((8, 128), 1) >> 5
    chunks = []
    for r in range(4):
        chunk = jnp.zeros((8, 128), f32)
        for t in range(4):
            part = attended[t * 8 : t * 8 + 8]
            if t != r:
                part = pltpu.roll(part, (t - r) % 4 * 32, 1)
            chunk = jnp.where(block == t, part, chunk)
        chunks.append(chunk)
    columns = jnp.concatenate(chunks, axis=1)
    high = iota((8, 512), 0) >= 4
    columns = jnp.concatenate(
        [jnp.where(high, 0.0, columns), jnp.where(high, columns, 0.0)], axis=1
    ).astype(bf16)
    update = lax.dot_general(columns, w_ref[...], NT, preferred_element_type=f32)
    update = update + pltpu.roll(update, 4, 0)
    first = iota((8, 128), 0) < 4
    own = jnp.where(first, tile_of(update, 0), tile_of(update, 1))
    other = jnp.where(first, tile_of(update, 2), tile_of(update, 3))
    same = info_ref[5] == 0
    blocks = [jnp.where(same, own, other), jnp.where(same, other, own)]
    copies = out_ref.shape[0] // 2
    for s in range(2):
        for j in range(copies):
            out_ref[s * copies + j] = blocks[s]


def updated(in_ref, hid_ref):
    update = total_of(in_ref)
    turned = pltpu.roll(update, 4, 0)
    first = iota((8, 128), 0) < 4
    update = jnp.concatenate(
        [jnp.where(first, update, turned), jnp.where(first, turned, update)], axis=1
    )
    return (hid_ref[...] + update).astype(bf16)


def next_kernel(in_ref, hid_ref, gain_ref, w_ref, new_ref, out_ref):
    hidden = updated(in_ref, hid_ref).astype(f32)
    new_ref[...] = hidden
    project(hidden, gain_ref[...], w_ref[...], out_ref)


def last_kernel(in_ref, hid_ref, out_ref):
    out_ref[...] = updated(in_ref, hid_ref)[:4]


def exchange(value, axes):
    return lax.all_to_all(value, axes, split_axis=0, concat_axis=0, tiled=True)


def shards(features, hidden_in, norm_gain, qkv_codes, qkv_scale, out_codes, out_scale,
           cache_keys, cache_values, lengths):
    near = lax.axis_size(NEAR)
    far = lax.axis_size(FAR)
    heads = lax.axis_size("head")
    gain = norm_gain.reshape(1, -1)
    batch, block_len = cache_keys.shape[:2]
    keys = cache_keys.reshape(batch, block_len, HEAD_DIM)
    values = cache_values.reshape(batch, block_len, HEAD_DIM)
    place = lax.axis_index(SEQ)
    low = lax.axis_index("z_low")
    info = jnp.concatenate(
        [lengths - place * block_len, jnp.stack([place, low]).astype(jnp.int32)]
    )
    wanted = lax.dynamic_slice_in_dim(out_codes, (1 - low) * 256, 256, axis=1)
    wanted = jnp.concatenate(
        [wanted.astype(f32), jnp.broadcast_to(out_scale[None, :], (8, 256))], axis=0
    )
    other = lax.ppermute(wanted, "z_low", [(0, 1), (1, 0)])

    half_dim = HEAD_DIM // 2
    freqs = jnp.exp(
        -(jnp.arange(half_dim, dtype=f32) * (2.0 / HEAD_DIM)) * math.log(ROPE_BASE)
    )
    steps = jnp.arange(DECODE_STEPS, dtype=jnp.int32)
    positions = lengths[None, :] + steps[:, None]
    angles = positions.astype(f32)[:, :, None] * freqs
    cosines, sines = jnp.cos(angles), jnp.sin(angles)
    cosines = jnp.tile(jnp.concatenate([cosines, cosines], axis=-1), (1, 2, 1))
    sines = jnp.tile(jnp.concatenate([-sines, sines], axis=-1), (1, 2, 1))

    w_qkv, hidden, partial = call(
        decode_qkv_kernel,
        (shape_of((2304, 256), bf16), shape_of((8, 256)), shape_of((near, 8, 640))),
        "decode_qkv",
        (hidden_in, gain, qkv_codes.T, qkv_scale.reshape(18, 128)),
    )
    w_out = call(
        decode_out_kernel,
        shape_of((512, 1024), bf16),
        "decode_out",
        (out_codes, out_scale.reshape(1, -1), other),
        (info,),
    )
    fresh = ()
    for step in range(DECODE_STEPS):
        partial = exchange(partial, NEAR)
        partial = call(pass_sum_kernel, shape_of((far, 8, 640)), "sum_near", (partial,))
        partial = exchange(partial, FAR)
        partial = call(pass_sum_kernel, shape_of((2, 8, 640)), "sum_far", (partial,))
        partial = exchange(partial, "z_low")
        part, new_key, new_value = call(
            functools.partial(attend_kernel, features, step),
            (shape_of((near, 8, 640)), shape_of((8, 128)), shape_of((8, 128))),
            "attend",
            (partial, cosines[step], sines[step], keys, values, *fresh),
            (info,),
        )
        fresh += (new_key, new_value)
        part = exchange(part, NEAR)
        part = call(pass_merge_kernel, shape_of((far, 8, 640)), "merge_near", (part,))
        part = exchange(part, FAR)
        update = call(
            finish_kernel, shape_of((2 * heads, 8, 128)), "finish", (part, w_out), (info,)
        )
        update = exchange(update, ("z_low", "head"))
        if step + 1 < DECODE_STEPS:
            hidden, partial = call(
                next_kernel,
                (shape_of((8, 256)), shape_of((near, 8, 640))),
                "next_step",
                (update, hidden, gain, w_qkv),
            )
    return call(last_kernel, shape_of((4, 256), bf16), "last", (update, hidden))


def solution(mesh):
    seq, head = mesh.shape["seq"], mesh.shape["head"]
    far = seq // 8
    split = Mesh(mesh.devices.reshape(far, 2, 4, head), (*SEQ, "head"))
    placed = (
        P(None, SEQ),
        P(SEQ),
        P(SEQ, "head"),
        P("head"),
        P(SEQ, "head"),
        P(SEQ),
        P(None, SEQ, "head", None),
        P(None, SEQ, "head", None),
        P(),
    )

    def run(hidden_in, *others):
        features = hidden_in.shape[1]
        return jax.shard_map(
            functools.partial(shards, float(features)),
            mesh=split,
            in_specs=placed,
            out_specs=P(None, SEQ),
            check_vma=False,
        )(hidden_in, *others)

    return run
```

```python
import functools
import math

import jax
import jax.numpy as jnp
from jax import lax
from jax.experimental import pallas as pl
from jax.experimental.pallas import tpu as pltpu
from jax.sharding import Mesh
from jax.sharding import PartitionSpec as P

HEAD_DIM = 128
GROUPS = 16
DECODE_STEPS = 2
NEAR = ("z_low", "y")
FAR = "z_high"
SEQ = (FAR, *NEAR)

CODE_NORM = 147.8
EPSILON = 1e-05
ROPE_BASE = 500000.0
SCORE_SCALE = HEAD_DIM ** (-0.5)

f32 = jnp.float32
bf16 = jnp.bfloat16
NT = (((1,), (1,)), ((), ()))


def iota(shape, axis):
    return lax.broadcasted_iota(jnp.int32, shape, axis)


def call(kernel, outs, name, arrays, scalars=(), remote=(), scratch=()):
    specs = [pl.BlockSpec(memory_space=pltpu.SMEM) for _ in scalars]
    specs += [pl.BlockSpec(memory_space=pltpu.HBM) for _ in remote]
    specs += [pl.BlockSpec(memory_space=pltpu.VMEM) for _ in arrays]
    remote = [pltpu.with_memory_space_constraint(x, pltpu.HBM) for x in remote]
    return pl.pallas_call(
        kernel,
        out_shape=outs,
        in_specs=specs,
        scratch_shapes=scratch,
        name=name,
        compiler_params=pltpu.CompilerParams(vmem_limit_bytes=16 * 1024 * 1024),
    )(*scalars, *remote, *arrays)


def shape_of(shape, dtype=f32):
    return jax.ShapeDtypeStruct(shape, dtype)


def byte_sum(state):
    x = state * 34038481 + 76625530
    pairs = (x & 0x00FF00FF) + ((x >> 8) & 0x00FF00FF)
    total = (pairs + (pairs >> 16)) & 0x7FF
    return (total - 510).astype(f32)


def interleave():
    row = iota((128, 128), 0)
    column = iota((128, 128), 1)
    return (column == 4 * (row & 31) + (row >> 5)).astype(f32).astype(bf16)


def by_sequence():
    row = iota((64, 64), 0)
    column = iota((64, 64), 1)
    return (column == 4 * (row & 15) + (row >> 4)).astype(f32).astype(bf16)


def by_place():
    row = iota((32, 32), 0)
    column = iota((32, 32), 1)
    source = 8 * (row & 3) + (row & 4) + (row >> 3)
    return (column == source).astype(f32).astype(bf16)


def exact_product(x, ones):
    rows = x.shape[0]
    high = x.astype(bf16).astype(f32)
    rest = x - high
    middle = rest.astype(bf16).astype(f32)
    low = rest - middle
    parts = jnp.concatenate([high, middle, low], axis=0).astype(bf16)
    product = jnp.dot(parts, ones, preferred_element_type=f32)
    return product[:rows] + product[rows : 2 * rows] + product[2 * rows :]


def tile_of(x, k):
    return x[:, k * 128 : k * 128 + 128]


def send_halves(out_ref, halves):
    copies = out_ref.shape[0] // 2
    for s in range(2):
        for j in range(copies):
            for k in range(5):
                out_ref[s * copies + j, :, k * 128 : k * 128 + 128] = halves[s][k]


def project(hidden, gain, weights, out_ref):
    squares = jnp.sum(hidden * hidden, axis=1, keepdims=True)
    normed = (hidden * gain).astype(bf16)
    y = lax.dot_general(normed, weights, NT, preferred_element_type=f32)
    first = iota((8, 128), 0) < 4
    spread = jnp.broadcast_to(squares, (8, 128))
    halves = []
    for s in range(2):
        tiles = [
            jnp.where(first, tile_of(y, 8 * s + 2 * i), tile_of(y, 8 * s + 2 * i + 1))
            for i in range(4)
        ]
        halves.append(tiles + [jnp.where(first, tile_of(y, 16 + s), spread)])
    send_halves(out_ref, halves)


def decode_qkv_kernel(codes_hbm, scale_hbm, gain_hbm, hidden_ref, w_ref, hid_ref, out_ref,
                      codes_ref, scale_ref, gain_ref, code_sems, scale_sem, gain_sem):
    chunks = code_sems.shape[0]
    chunk_rows = codes_ref.shape[0] // chunks
    copies = []
    for i in range(chunks):
        rows = pl.ds(i * chunk_rows, chunk_rows)
        copies.append(
            pltpu.make_async_copy(codes_hbm.at[rows], codes_ref.at[rows], code_sems.at[i])
        )
    scale_copy = pltpu.make_async_copy(scale_hbm, scale_ref, scale_sem)
    gain_copy = pltpu.make_async_copy(gain_hbm, gain_ref, gain_sem)
    scale_copy.start()
    for copy in copies:
        copy.start()
    gain_copy.start()
    scale_copy.wait()
    lane = iota((32, 128), 1)
    word = iota((32, 128), 0)
    for tile in range(18):
        if tile * 32 % chunk_rows == 0:
            copies[tile * 32 // chunk_rows].wait()
        codes = codes_ref[tile * 32 : tile * 32 + 32, :]
        window = (codes << 16) | (pltpu.roll(codes, 31, 0) << 8) | pltpu.roll(codes, 30, 0)
        scales = jnp.broadcast_to(scale_ref[tile : tile + 1, :], (32, 128)) * (1.0 / CODE_NORM)
        for r in range(4):
            column = jnp.sum(
                jnp.where(lane == 4 * word + r, scales, 0.0), axis=1, keepdims=True
            )
            values = byte_sum((window >> (8 - 2 * r)) & 0xFFFF) * column
            at = tile * 128 + r * 32
            w_ref[at : at + 32, :] = values.astype(bf16)
    hidden = hidden_ref[...].astype(f32)
    hidden = jnp.concatenate([hidden, hidden], axis=0)
    hid_ref[...] = hidden
    gain_copy.wait()
    project(hidden, gain_ref[...], w_ref[...], out_ref)


def decode_out_kernel(info_ref, codes_ref, scale_ref, other_ref, w_ref):
    s = info_ref[5]
    lane = iota((32, 128), 1)
    within = lane & 31
    for block in range(16):
        own = block < 8
        rows = slice(block % 8 * 32, block % 8 * 32 + 32)
        across = iota((32, 256), 1) == iota((32, 256), 0) + block % 8 * 32
        scale = scale_ref[...] if own else other_ref[256:257, :]
        scale = jnp.broadcast_to(scale, (32, 256)) * (1.0 / CODE_NORM)
        column = jnp.sum(jnp.where(across, scale, 0.0), axis=1, keepdims=True)
        for group in range(2):
            if own:
                codes = jnp.where(
                    s == 0,
                    codes_ref[rows, group * 128 : group * 128 + 128],
                    codes_ref[rows, group * 128 + 256 : group * 128 + 384],
                )
            else:
                codes = other_ref[rows, group * 128 : group * 128 + 128].astype(jnp.int32)
            second = jnp.where(within < 31, pltpu.roll(codes, 127, 1), pltpu.roll(codes, 31, 1))
            third = jnp.where(within < 30, pltpu.roll(codes, 126, 1), pltpu.roll(codes, 30, 1))
            window = (codes << 16) | (second << 8) | third
            for r in range(4):
                values = byte_sum((window >> (8 - 2 * r)) & 0xFFFF) * column
                at = group * 512 + r * 128
                w_ref[block * 32 : block * 32 + 32, at : at + 128] = values.astype(bf16)


def total_of(ref):
    total = ref[0]
    for j in range(1, ref.shape[0]):
        total = total + ref[j]
    return total


def pass_sum_kernel(in_ref, out_ref):
    total = total_of(in_ref)
    for j in range(out_ref.shape[0]):
        out_ref[j] = total


def merged(in_ref):
    parts = range(in_ref.shape[0])
    stats = [in_ref[j, :, 512:] for j in parts]
    top = functools.reduce(jnp.maximum, stats)
    factors = [jnp.exp(x - top) for x in stats]
    sums = stats[0] * pltpu.roll(factors[0], 4, 1)
    for j in parts[1:]:
        sums = sums + stats[j] * pltpu.roll(factors[j], 4, 1)
    accs = []
    for b in range(4):
        at = slice(b * 128, b * 128 + 128)
        acc = in_ref[0, :, at] * factors[0][:, b : b + 1]
        for j in parts[1:]:
            acc = acc + in_ref[j, :, at] * factors[j][:, b : b + 1]
        accs.append(acc)
    return top, sums, accs


def pass_merge_kernel(in_ref, out_ref):
    top, sums, accs = merged(in_ref)
    lane = iota((8, 128), 1)
    stats = jnp.where(lane < 4, top, jnp.where(lane < 8, sums, 0.0))
    for j in range(out_ref.shape[0]):
        for b in range(4):
            out_ref[j, :, b * 128 : b * 128 + 128] = accs[b]
        out_ref[j, :, 512:] = stats


def attend_kernel(features, earlier, info_ref, keys_hbm, values_hbm, in_ref, cos_ref, sin_ref,
                  *refs):
    out_ref, k_ref, v_ref, keys_ref, values_ref, key_sems, value_sems = refs[2 * earlier :]
    key_copies = [
        pltpu.make_async_copy(keys_hbm.at[b], keys_ref.at[b], key_sems.at[b]) for b in range(4)
    ]
    value_copies = [
        pltpu.make_async_copy(values_hbm.at[b], values_ref.at[b], value_sems.at[b])
        for b in range(4)
    ]
    for b in range(4):
        key_copies[b].start()
        value_copies[b].start()
    first = iota((8, 128), 0) < 4
    last = in_ref[0, :, 512:]
    squares = jnp.where(first, pltpu.roll(last, 4, 0), last)
    rms = lax.rsqrt(squares / features + EPSILON)
    tiles = [tile_of(in_ref[s], i) * rms for s in range(2) for i in range(4)]
    tiles += [in_ref[s, :, 512:] * rms for s in range(2)]
    x = exact_product(jnp.concatenate(tiles, axis=0), interleave())
    cos = jnp.concatenate([cos_ref[...]] * 18, axis=0)
    sin = jnp.concatenate([sin_ref[...]] * 18, axis=0)
    turned = x[:72] * cos + pltpu.roll(x[:72], 64, 1) * sin
    turned = turned.astype(bf16)
    new_key = turned[64:72].astype(f32)
    new_value = x[72:].astype(bf16).astype(f32)
    k_ref[...] = new_key
    v_ref[...] = new_value
    queries = jnp.dot(by_sequence(), turned[:64], preferred_element_type=f32)
    new_keys = [refs[2 * u][...] for u in range(earlier)] + [new_key]
    new_values = [refs[2 * u + 1][...] for u in range(earlier)] + [new_value]
    owner = info_ref[4] == 0
    length = keys_ref.shape[1]
    place = iota((16, length), 1)
    lane = iota((8, 128), 1)
    halves = [[], []]
    stats = [jnp.zeros((8, 128), f32)] * 2
    for b in range(4):
        query = queries[b * 16 : b * 16 + 16]
        key_copies[b].wait()
        scores = lax.dot_general(
            query.astype(bf16), keys_ref[b], NT, preferred_element_type=f32
        ) * SCORE_SCALE
        live = place < info_ref[b]
        top = jnp.max(jnp.where(live, scores, -1e30), axis=1, keepdims=True)
        weights = jnp.where(live, jnp.exp(scores - top), 0.0)
        total = jnp.sum(weights, axis=1, keepdims=True)
        value_copies[b].wait()
        acc = jnp.dot(weights.astype(bf16), values_ref[b], preferred_element_type=f32)
        fresh = [
            jnp.where(
                owner,
                jnp.sum(query * key[b : b + 1, :], axis=1, keepdims=True) * SCORE_SCALE,
                -1e30,
            )
            for key in new_keys
        ]
        peak = functools.reduce(jnp.maximum, fresh, top)
        factor = jnp.exp(top - peak)
        total = total * factor
        acc = acc * factor
        for score, value in zip(fresh, new_values):
            weight = jnp.where(owner, jnp.exp(score - peak), 0.0)
            total = total + weight
            acc = acc + weight * value[b : b + 1, :]
        for s in range(2):
            rows = slice(8 * s, 8 * s + 8)
            halves[s].append(acc[rows])
            stats[s] = jnp.where(lane == b, peak[rows], stats[s])
            stats[s] = jnp.where(lane == 4 + b, total[rows], stats[s])
    send_halves(out_ref, [halves[s] + [stats[s]] for s in range(2)])


def finish_kernel(info_ref, in_ref, w_ref, out_ref):
    _, sums, accs = merged(in_ref)
    attended = jnp.concatenate(
        [accs[b] / sums[:, 4 + b : 5 + b] for b in range(4)], axis=0
    ).astype(bf16)
    attended = jnp.dot(by_place(), attended, preferred_element_type=f32).astype(bf16)
    attended = lax.dot_general(attended, interleave(), NT, preferred_element_type=f32)
    block = iota((8, 128), 1) >> 5
    chunks = []
    for r in range(4):
        chunk = jnp.zeros((8, 128), f32)
        for t in range(4):
            part = attended[t * 8 : t * 8 + 8]
            if t != r:
                part = pltpu.roll(part, (t - r) % 4 * 32, 1)
            chunk = jnp.where(block == t, part, chunk)
        chunks.append(chunk)
    columns = jnp.concatenate(chunks, axis=1)
    high = iota((8, 512), 0) >= 4
    columns = jnp.concatenate(
        [jnp.where(high, 0.0, columns), jnp.where(high, columns, 0.0)], axis=1
    ).astype(bf16)
    update = lax.dot_general(columns, w_ref[...], NT, preferred_element_type=f32)
    update = update + pltpu.roll(update, 4, 0)
    first = iota((8, 128), 0) < 4
    own = jnp.where(first, tile_of(update, 0), tile_of(update, 1))
    other = jnp.where(first, tile_of(update, 2), tile_of(update, 3))
    same = info_ref[5] == 0
    blocks = [jnp.where(same, own, other), jnp.where(same, other, own)]
    copies = out_ref.shape[0] // 2
    for s in range(2):
        for j in range(copies):
            out_ref[s * copies + j] = blocks[s]


def updated(in_ref, hid_ref):
    update = total_of(in_ref)
    turned = pltpu.roll(update, 4, 0)
    first = iota((8, 128), 0) < 4
    update = jnp.concatenate(
        [jnp.where(first, update, turned), jnp.where(first, turned, update)], axis=1
    )
    return (hid_ref[...] + update).astype(bf16)


def next_kernel(in_ref, hid_ref, gain_ref, w_ref, new_ref, out_ref):
    hidden = updated(in_ref, hid_ref).astype(f32)
    new_ref[...] = hidden
    project(hidden, gain_ref[...], w_ref[...], out_ref)


def last_kernel(in_ref, hid_ref, out_ref):
    out_ref[...] = updated(in_ref, hid_ref)[:4]


def exchange(value, axes):
    return lax.all_to_all(value, axes, split_axis=0, concat_axis=0, tiled=True)


def shards(features, hidden_in, norm_gain, qkv_codes, qkv_scale, out_codes, out_scale,
           cache_keys, cache_values, lengths):
    near = lax.axis_size(NEAR)
    far = lax.axis_size(FAR)
    heads = lax.axis_size("head")
    gain = norm_gain.reshape(1, -1)
    batch, block_len = cache_keys.shape[:2]
    keys = cache_keys.reshape(batch, block_len, HEAD_DIM)
    values = cache_values.reshape(batch, block_len, HEAD_DIM)
    place = lax.axis_index(SEQ)
    low = lax.axis_index("z_low")
    info = jnp.concatenate(
        [lengths - place * block_len, jnp.stack([place, low]).astype(jnp.int32)]
    )
    wanted = lax.dynamic_slice_in_dim(out_codes, (1 - low) * 256, 256, axis=1)
    wanted = jnp.concatenate(
        [wanted.astype(f32), jnp.broadcast_to(out_scale[None, :], (8, 256))], axis=0
    )
    other = lax.ppermute(wanted, "z_low", [(0, 1), (1, 0)])

    half_dim = HEAD_DIM // 2
    freqs = jnp.exp(
        -(jnp.arange(half_dim, dtype=f32) * (2.0 / HEAD_DIM)) * math.log(ROPE_BASE)
    )
    steps = jnp.arange(DECODE_STEPS, dtype=jnp.int32)
    positions = lengths[None, :] + steps[:, None]
    angles = positions.astype(f32)[:, :, None] * freqs
    cosines, sines = jnp.cos(angles), jnp.sin(angles)
    cosines = jnp.concatenate([cosines, cosines], axis=-1)
    sines = jnp.concatenate([-sines, sines], axis=-1)

    w_qkv, hidden, partial = call(
        decode_qkv_kernel,
        (shape_of((2304, 256), bf16), shape_of((8, 256)), shape_of((near, 8, 640))),
        "decode_qkv",
        (hidden_in,),
        remote=(qkv_codes.T, qkv_scale.reshape(18, 128), gain),
        scratch=(
            pltpu.VMEM((576, 256), jnp.int32),
            pltpu.VMEM((18, 128), f32),
            pltpu.VMEM((1, 256), f32),
            pltpu.SemaphoreType.DMA((6,)),
            pltpu.SemaphoreType.DMA,
            pltpu.SemaphoreType.DMA,
        ),
    )
    fresh = ()
    for step in range(DECODE_STEPS):
        partial = exchange(partial, NEAR)
        if step == 0:
            partial, other = lax.optimization_barrier((partial, other))
            w_out = call(
                decode_out_kernel,
                shape_of((512, 1024), bf16),
                "decode_out",
                (out_codes, out_scale.reshape(1, -1), other),
                (info,),
            )
        partial = call(pass_sum_kernel, shape_of((far, 8, 640)), "sum_near", (partial,))
        partial = exchange(partial, FAR)
        partial = call(pass_sum_kernel, shape_of((2, 8, 640)), "sum_far", (partial,))
        partial = exchange(partial, "z_low")
        part, new_key, new_value = call(
            functools.partial(attend_kernel, features, step),
            (shape_of((near, 8, 640)), shape_of((8, 128)), shape_of((8, 128))),
            "attend",
            (partial, cosines[step], sines[step], *fresh),
            (info,),
            (keys, values),
            (
                pltpu.VMEM(keys.shape, bf16),
                pltpu.VMEM(keys.shape, bf16),
                pltpu.SemaphoreType.DMA((4,)),
                pltpu.SemaphoreType.DMA((4,)),
            ),
        )
        fresh += (new_key, new_value)
        part = exchange(part, NEAR)
        part = call(pass_merge_kernel, shape_of((far, 8, 640)), "merge_near", (part,))
        part = exchange(part, FAR)
        update = call(
            finish_kernel, shape_of((2 * heads, 8, 128)), "finish", (part, w_out), (info,)
        )
        update = exchange(update, ("z_low", "head"))
        if step + 1 < DECODE_STEPS:
            hidden, partial = call(
                next_kernel,
                (shape_of((8, 256)), shape_of((near, 8, 640))),
                "next_step",
                (update, hidden, gain, w_qkv),
            )
    return call(last_kernel, shape_of((4, 256), bf16), "last", (update, hidden))


def solution(mesh):
    seq, head = mesh.shape["seq"], mesh.shape["head"]
    far = seq // 8
    split = Mesh(mesh.devices.reshape(far, 2, 4, head), (*SEQ, "head"))
    placed = (
        P(None, SEQ),
        P(SEQ),
        P(SEQ, "head"),
        P("head"),
        P(SEQ, "head"),
        P(SEQ),
        P(None, SEQ, "head", None),
        P(None, SEQ, "head", None),
        P(),
    )

    def run(hidden_in, *others):
        features = hidden_in.shape[1]
        return jax.shard_map(
            functools.partial(shards, float(features)),
            mesh=split,
            in_specs=placed,
            out_specs=P(None, SEQ),
            check_vma=False,
        )(hidden_in, *others)

    return run
```

```python
import functools
import math

import jax
import jax.numpy as jnp
from jax import lax
from jax.experimental import pallas as pl
from jax.experimental.pallas import tpu as pltpu
from jax.sharding import Mesh
from jax.sharding import PartitionSpec as P

HEAD_DIM = 128
GROUPS = 16
DECODE_STEPS = 2
NEAR = ("z_low", "y")
FAR = "z_high"
Z = ("z_high", "z_low")
SEQ = (FAR, *NEAR)

CODE_NORM = 147.8
EPSILON = 1e-05
ROPE_BASE = 500000.0
SCORE_SCALE = HEAD_DIM ** (-0.5)

f32 = jnp.float32
bf16 = jnp.bfloat16
NT = (((1,), (1,)), ((), ()))


def iota(shape, axis):
    return lax.broadcasted_iota(jnp.int32, shape, axis)


def call(kernel, outs, name, arrays, scalars=(), remote=(), scratch=(), out_specs=None):
    specs = [pl.BlockSpec(memory_space=pltpu.SMEM) for _ in scalars]
    specs += [pl.BlockSpec(memory_space=pltpu.HBM) for _ in remote]
    specs += [pl.BlockSpec(memory_space=pltpu.VMEM) for _ in arrays]
    remote = [pltpu.with_memory_space_constraint(x, pltpu.HBM) for x in remote]
    return pl.pallas_call(
        kernel,
        out_shape=outs,
        in_specs=specs,
        out_specs=out_specs or jax.tree.map(lambda _: pl.BlockSpec(memory_space=pltpu.VMEM), outs),
        scratch_shapes=scratch,
        name=name,
        compiler_params=pltpu.CompilerParams(vmem_limit_bytes=16 * 1024 * 1024),
    )(*scalars, *remote, *arrays)


def shape_of(shape, dtype=f32):
    return jax.ShapeDtypeStruct(shape, dtype)


def byte_sum(state):
    x = state * 34038481 + 76625530
    pairs = (x & 0x00FF00FF) + ((x >> 8) & 0x00FF00FF)
    total = (pairs + (pairs >> 16)) & 0x7FF
    return (total - 510).astype(f32)


def interleave():
    row = iota((128, 128), 0)
    column = iota((128, 128), 1)
    return (column == 4 * (row & 31) + (row >> 5)).astype(f32).astype(bf16)


def exact_product(x, ones):
    rows = x.shape[0]
    high = x.astype(bf16).astype(f32)
    rest = x - high
    middle = rest.astype(bf16).astype(f32)
    low = rest - middle
    parts = jnp.concatenate([high, middle, low], axis=0).astype(bf16)
    product = jnp.dot(parts, ones, preferred_element_type=f32)
    return product[:rows] + product[rows : 2 * rows] + product[2 * rows :]


def tile_of(x, k):
    return x[:, k * 128 : k * 128 + 128]


def send_halves(out_ref, halves):
    copies = out_ref.shape[0] // 2
    for s in range(2):
        for j in range(copies):
            for k in range(5):
                out_ref[s * copies + j, :, k * 128 : k * 128 + 128] = halves[s][k]


def project(hidden, gain, weights, out_ref):
    squares = jnp.sum(hidden * hidden, axis=1, keepdims=True)
    normed = (hidden * gain).astype(bf16)
    y = lax.dot_general(normed, weights, NT, preferred_element_type=f32)
    first = iota((8, 128), 0) < 4
    spread = jnp.broadcast_to(squares, (8, 128))
    halves = []
    for s in range(2):
        tiles = [
            jnp.where(first, tile_of(y, 8 * s + 2 * i), tile_of(y, 8 * s + 2 * i + 1))
            for i in range(4)
        ]
        halves.append(tiles + [jnp.where(first, tile_of(y, 16 + s), spread)])
    send_halves(out_ref, halves)


def decode_qkv_kernel(codes_hbm, scale_hbm, gain_hbm, hidden_ref, w_hbm, hid_ref, out_ref,
                      codes_ref, scale_ref, gain_ref, w_ref, code_sems, scale_sem, gain_sem,
                      w_sems):
    chunks = code_sems.shape[0]
    chunk_rows = codes_ref.shape[0] // chunks
    copies = []
    for i in range(chunks):
        rows = pl.ds(i * chunk_rows, chunk_rows)
        copies.append(
            pltpu.make_async_copy(codes_hbm.at[rows], codes_ref.at[rows], code_sems.at[i])
        )
    scale_copy = pltpu.make_async_copy(scale_hbm, scale_ref, scale_sem)
    gain_copy = pltpu.make_async_copy(gain_hbm, gain_ref, gain_sem)
    scale_copy.start()
    for copy in copies:
        copy.start()
    gain_copy.start()
    scale_copy.wait()
    lane = iota((32, 128), 1)
    word = iota((32, 128), 0)
    kept = []
    for tile in range(18):
        if tile * 32 % chunk_rows == 0:
            copies[tile * 32 // chunk_rows].wait()
        codes = codes_ref[tile * 32 : tile * 32 + 32, :]
        window = (codes << 16) | (pltpu.roll(codes, 31, 0) << 8) | pltpu.roll(codes, 30, 0)
        scales = jnp.broadcast_to(scale_ref[tile : tile + 1, :], (32, 128)) * (1.0 / CODE_NORM)
        for r in range(4):
            column = jnp.sum(
                jnp.where(lane == 4 * word + r, scales, 0.0), axis=1, keepdims=True
            )
            values = byte_sum((window >> (8 - 2 * r)) & 0xFFFF) * column
            at = tile * 128 + r * 32
            w_ref[at : at + 32, :] = values.astype(bf16)
        if (tile + 1) * 32 % chunk_rows == 0:
            done = tile * 32 // chunk_rows
            rows = pl.ds(done * 4 * chunk_rows, 4 * chunk_rows)
            kept.append(pltpu.make_async_copy(w_ref.at[rows], w_hbm.at[rows], w_sems.at[done]))
            kept[-1].start()
    hidden = hidden_ref[...].astype(f32)
    hidden = jnp.concatenate([hidden, hidden], axis=0)
    hid_ref[...] = hidden
    gain_copy.wait()
    project(hidden, gain_ref[...], w_ref[...], out_ref)
    for copy in kept:
        copy.wait()


def decode_out_kernel(info_ref, codes_ref, scale_ref, other_ref, w_ref):
    s = info_ref[5]
    lane = iota((32, 128), 1)
    within = lane & 31
    for block in range(16):
        own = block < 8
        rows = slice(block % 8 * 32, block % 8 * 32 + 32)
        across = iota((32, 256), 1) == iota((32, 256), 0) + block % 8 * 32
        scale = scale_ref[...] if own else other_ref[256:257, :]
        scale = jnp.broadcast_to(scale, (32, 256)) * (1.0 / CODE_NORM)
        column = jnp.sum(jnp.where(across, scale, 0.0), axis=1, keepdims=True)
        for group in range(2):
            if own:
                codes = jnp.where(
                    s == 0,
                    codes_ref[rows, group * 128 : group * 128 + 128],
                    codes_ref[rows, group * 128 + 256 : group * 128 + 384],
                )
            else:
                codes = other_ref[rows, group * 128 : group * 128 + 128].astype(jnp.int32)
            second = jnp.where(within < 31, pltpu.roll(codes, 127, 1), pltpu.roll(codes, 31, 1))
            third = jnp.where(within < 30, pltpu.roll(codes, 126, 1), pltpu.roll(codes, 30, 1))
            window = (codes << 16) | (second << 8) | third
            for r in range(4):
                values = byte_sum((window >> (8 - 2 * r)) & 0xFFFF) * column
                at = group * 512 + r * 128
                w_ref[block * 32 : block * 32 + 32, at : at + 128] = values.astype(bf16)


def total_of(ref):
    total = ref[0]
    for j in range(1, ref.shape[0]):
        total = total + ref[j]
    return total


def pass_sum_kernel(in_ref, out_ref):
    total = total_of(in_ref)
    for j in range(out_ref.shape[0]):
        out_ref[j] = total


def merged(in_ref):
    parts = range(in_ref.shape[0])
    stats = [in_ref[j, :, 512:] for j in parts]
    top = functools.reduce(jnp.maximum, stats)
    factors = [jnp.exp(x - top) for x in stats]
    sums = stats[0] * pltpu.roll(factors[0], 4, 1)
    for j in parts[1:]:
        sums = sums + stats[j] * pltpu.roll(factors[j], 4, 1)
    accs = []
    for b in range(4):
        at = slice(b * 128, b * 128 + 128)
        acc = in_ref[0, :, at] * factors[0][:, b : b + 1]
        for j in parts[1:]:
            acc = acc + in_ref[j, :, at] * factors[j][:, b : b + 1]
        accs.append(acc)
    return top, sums, accs


def pass_merge_kernel(in_ref, out_ref):
    top, sums, accs = merged(in_ref)
    lane = iota((8, 128), 1)
    stats = jnp.where(lane < 4, top, jnp.where(lane < 8, sums, 0.0))
    for j in range(out_ref.shape[0]):
        for b in range(4):
            out_ref[j, :, b * 128 : b * 128 + 128] = accs[b]
        out_ref[j, :, 512:] = stats


def attend_kernel(features, earlier, info_ref, in_ref, cos_ref, sin_ref, keys_ref, values_ref,
                  *refs):
    out_ref, k_ref, v_ref, q_ref = refs[2 * earlier :]
    halves = []
    for s in range(2):
        total = in_ref[s]
        for j in range(2 + s, in_ref.shape[0], 2):
            total = total + in_ref[j]
        halves.append(total)
    first = iota((8, 128), 0) < 4
    last = tile_of(halves[0], 4)
    squares = jnp.where(first, pltpu.roll(last, 4, 0), last)
    rms = lax.rsqrt(squares / features + EPSILON)
    tiles = [tile_of(half, i) * rms for half in halves for i in range(4)]
    tiles += [tile_of(half, 4) * rms for half in halves]
    x = exact_product(jnp.concatenate(tiles, axis=0), interleave())
    cos = jnp.concatenate([cos_ref[...]] * 18, axis=0)
    sin = jnp.concatenate([sin_ref[...]] * 18, axis=0)
    turned = x[:72] * cos + pltpu.roll(x[:72], 64, 1) * sin
    turned = turned.astype(bf16).astype(f32)
    q_ref[...] = turned[:64]
    new_key = turned[64:]
    new_value = x[72:].astype(bf16).astype(f32)
    k_ref[...] = new_key
    v_ref[...] = new_value
    new_keys = [refs[2 * u][...] for u in range(earlier)] + [new_key]
    new_values = [refs[2 * u + 1][...] for u in range(earlier)] + [new_value]
    owner = info_ref[4] == 0
    length = keys_ref.shape[1]
    place = iota((16, length), 1)
    lane = iota((8, 128), 1)
    halves = [[], []]
    stats = [jnp.zeros((8, 128), f32)] * 2
    for b in range(4):
        query = q_ref[pl.ds(b, 16, stride=4), :]
        scores = lax.dot_general(
            query.astype(bf16), keys_ref[b], NT, preferred_element_type=f32
        ) * SCORE_SCALE
        live = place < info_ref[b]
        top = jnp.max(jnp.where(live, scores, -1e30), axis=1, keepdims=True)
        weights = jnp.where(live, jnp.exp(scores - top), 0.0)
        total = jnp.sum(weights, axis=1, keepdims=True)
        acc = jnp.dot(weights.astype(bf16), values_ref[b], preferred_element_type=f32)
        fresh = [
            jnp.where(
                owner,
                jnp.sum(query * key[b : b + 1, :], axis=1, keepdims=True) * SCORE_SCALE,
                -1e30,
            )
            for key in new_keys
        ]
        peak = functools.reduce(jnp.maximum, fresh, top)
        factor = jnp.exp(top - peak)
        total = total * factor
        acc = acc * factor
        for score, value in zip(fresh, new_values):
            weight = jnp.where(owner, jnp.exp(score - peak), 0.0)
            total = total + weight
            acc = acc + weight * value[b : b + 1, :]
        for s in range(2):
            rows = slice(8 * s, 8 * s + 8)
            halves[s].append(acc[rows])
            stats[s] = jnp.where(lane == b, peak[rows], stats[s])
            stats[s] = jnp.where(lane == 4 + b, total[rows], stats[s])
    send_halves(out_ref, [halves[s] + [stats[s]] for s in range(2)])


def finish_kernel(info_ref, in_ref, w_ref, out_ref, rows_ref):
    _, sums, accs = merged(in_ref)
    for b in range(4):
        attended = (accs[b] / sums[:, 4 + b : 5 + b]).astype(bf16).astype(f32)
        rows_ref[b * 8 : b * 8 + 8, :] = attended
        rows_ref[b * 8 + 32 : b * 8 + 40, :] = attended
    attended = jnp.concatenate(
        [rows_ref[pl.ds(t, 8, stride=8), :] for t in range(8)], axis=0
    ).astype(bf16)
    attended = lax.dot_general(attended, interleave(), NT, preferred_element_type=f32)
    block = iota((8, 128), 1) >> 5
    chunks = []
    for group in range(2):
        for r in range(4):
            chunk = jnp.zeros((8, 128), f32)
            for t in range(4):
                at = (group * 4 + t) * 8
                part = attended[at : at + 8]
                if t != r:
                    part = pltpu.roll(part, (t - r) % 4 * 32, 1)
                chunk = jnp.where(block == t, part, chunk)
            chunks.append(chunk)
    columns = jnp.concatenate(chunks, axis=1).astype(bf16)
    update = lax.dot_general(columns, w_ref[...], NT, preferred_element_type=f32)
    first = iota((8, 128), 0) < 4
    own = jnp.where(first, tile_of(update, 0), tile_of(update, 1))
    other = jnp.where(first, tile_of(update, 2), tile_of(update, 3))
    same = info_ref[5] == 0
    blocks = [jnp.where(same, own, other), jnp.where(same, other, own)]
    copies = out_ref.shape[0] // 2
    for s in range(2):
        for j in range(copies):
            out_ref[s * copies + j] = blocks[s]


def updated(in_ref, hid_ref):
    update = total_of(in_ref)
    turned = pltpu.roll(update, 4, 0)
    first = iota((8, 128), 0) < 4
    update = jnp.concatenate(
        [jnp.where(first, update, turned), jnp.where(first, turned, update)], axis=1
    )
    return (hid_ref[...] + update).astype(bf16)


def next_kernel(in_ref, hid_ref, gain_ref, w_ref, new_ref, out_ref):
    hidden = updated(in_ref, hid_ref).astype(f32)
    new_ref[...] = hidden
    project(hidden, gain_ref[...], w_ref[...], out_ref)


def last_kernel(in_ref, hid_ref, out_ref):
    out_ref[...] = updated(in_ref, hid_ref)[:4]


def exchange(value, axes):
    return lax.all_to_all(value, axes, split_axis=0, concat_axis=0, tiled=True)


def shards(features, hidden_in, norm_gain, qkv_codes, qkv_scale, out_codes, out_scale,
           cache_keys, cache_values, lengths):
    near = lax.axis_size(NEAR)
    far = lax.axis_size(FAR)
    heads = lax.axis_size("head")
    gain = norm_gain.reshape(1, -1)
    batch, block_len = cache_keys.shape[:2]
    keys = cache_keys.reshape(batch, block_len, HEAD_DIM)
    values = cache_values.reshape(batch, block_len, HEAD_DIM)
    place = lax.axis_index(SEQ)
    low = lax.axis_index("z_low")
    info = jnp.concatenate(
        [lengths - place * block_len, jnp.stack([place, low]).astype(jnp.int32)]
    )
    wanted = lax.dynamic_slice_in_dim(out_codes, (1 - low) * 256, 256, axis=1)
    wanted = jnp.concatenate(
        [wanted.astype(f32), jnp.broadcast_to(out_scale[None, :], (8, 256))], axis=0
    )
    other = lax.ppermute(wanted, "z_low", [(0, 1), (1, 0)])

    half_dim = HEAD_DIM // 2
    freqs = jnp.exp(
        -(jnp.arange(half_dim, dtype=f32) * (2.0 / HEAD_DIM)) * math.log(ROPE_BASE)
    )
    steps = jnp.arange(DECODE_STEPS, dtype=jnp.int32)
    positions = lengths[None, :] + steps[:, None]
    angles = positions.astype(f32)[:, :, None] * freqs
    cosines, sines = jnp.cos(angles), jnp.sin(angles)
    cosines = jnp.concatenate([cosines, cosines], axis=-1)
    sines = jnp.concatenate([-sines, sines], axis=-1)
    cosines = tuple(cosines[step] for step in range(DECODE_STEPS))
    sines = tuple(sines[step] for step in range(DECODE_STEPS))

    w_qkv, hidden, partial = call(
        decode_qkv_kernel,
        (pltpu.HBM((2304, 256), bf16), shape_of((8, 256)), shape_of((near, 8, 640))),
        "decode_qkv",
        (hidden_in,),
        remote=(qkv_codes.T, qkv_scale.reshape(18, 128), gain),
        scratch=(
            pltpu.VMEM((576, 256), jnp.int32),
            pltpu.VMEM((18, 128), f32),
            pltpu.VMEM((1, 256), f32),
            pltpu.VMEM((2304, 256), bf16),
            pltpu.SemaphoreType.DMA((6,)),
            pltpu.SemaphoreType.DMA,
            pltpu.SemaphoreType.DMA,
            pltpu.SemaphoreType.DMA((6,)),
        ),
        out_specs=(
            pl.BlockSpec(memory_space=pltpu.HBM),
            pl.BlockSpec(memory_space=pltpu.VMEM),
            pl.BlockSpec(memory_space=pltpu.VMEM),
        ),
    )
    fresh = ()
    for step in range(DECODE_STEPS):
        partial = exchange(partial, NEAR)
        if step == 0:
            partial, other, info, cosines, sines = lax.optimization_barrier(
                (partial, other, info, cosines, sines)
            )
            w_out = call(
                decode_out_kernel,
                shape_of((512, 1024), bf16),
                "decode_out",
                (out_codes, out_scale.reshape(1, -1), other),
                (info,),
            )
        partial = call(pass_sum_kernel, shape_of((2 * far, 8, 640)), "sum_near", (partial,))
        partial = exchange(partial, Z)
        part, new_key, new_value = call(
            functools.partial(attend_kernel, features, step),
            (shape_of((near, 8, 640)), shape_of((8, 128)), shape_of((8, 128))),
            "attend",
            (partial, cosines[step], sines[step], keys, values, *fresh),
            (info,),
            scratch=(pltpu.VMEM((64, 128), f32),),
        )
        fresh += (new_key, new_value)
        part = exchange(part, NEAR)
        part = call(pass_merge_kernel, shape_of((far, 8, 640)), "merge_near", (part,))
        part = exchange(part, FAR)
        update = call(
            finish_kernel,
            shape_of((2 * heads, 8, 128)),
            "finish",
            (part, w_out),
            (info,),
            scratch=(pltpu.VMEM((64, 128), f32),),
        )
        update = exchange(update, ("z_low", "head"))
        if step + 1 < DECODE_STEPS:
            hidden, partial = call(
                next_kernel,
                (shape_of((8, 256)), shape_of((near, 8, 640))),
                "next_step",
                (update, hidden, gain, w_qkv),
            )
    return call(last_kernel, shape_of((4, 256), bf16), "last", (update, hidden))


def solution(mesh):
    seq, head = mesh.shape["seq"], mesh.shape["head"]
    far = seq // 8
    split = Mesh(mesh.devices.reshape(far, 2, 4, head), (*SEQ, "head"))
    placed = (
        P(None, SEQ),
        P(SEQ),
        P(SEQ, "head"),
        P("head"),
        P(SEQ, "head"),
        P(SEQ),
        P(None, SEQ, "head", None),
        P(None, SEQ, "head", None),
        P(),
    )

    def run(hidden_in, *others):
        features = hidden_in.shape[1]
        return jax.shard_map(
            functools.partial(shards, float(features)),
            mesh=split,
            in_specs=placed,
            out_specs=P(None, SEQ),
            check_vma=False,
        )(hidden_in, *others)

    return run
```

```python
import functools
import math

import jax
import jax.numpy as jnp
from jax import lax
from jax.experimental import pallas as pl
from jax.experimental.pallas import tpu as pltpu
from jax.sharding import Mesh
from jax.sharding import PartitionSpec as P

HEAD_DIM = 128
GROUPS = 16
DECODE_STEPS = 2
NEAR = ("z_low", "y")
FAR = "z_high"
SEQ = (FAR, *NEAR)

CODE_NORM = 147.8
EPSILON = 1e-05
ROPE_BASE = 500000.0
SCORE_SCALE = HEAD_DIM ** (-0.5)

f32 = jnp.float32
bf16 = jnp.bfloat16
NT = (((1,), (1,)), ((), ()))


def iota(shape, axis):
    return lax.broadcasted_iota(jnp.int32, shape, axis)


def call(kernel, outs, name, arrays, scalars=(), remote=(), scratch=(), out_specs=None):
    specs = [pl.BlockSpec(memory_space=pltpu.SMEM) for _ in scalars]
    specs += [pl.BlockSpec(memory_space=pltpu.HBM) for _ in remote]
    specs += [pl.BlockSpec(memory_space=pltpu.VMEM) for _ in arrays]
    remote = [pltpu.with_memory_space_constraint(x, pltpu.HBM) for x in remote]
    return pl.pallas_call(
        kernel,
        out_shape=outs,
        in_specs=specs,
        out_specs=out_specs or jax.tree.map(lambda _: pl.BlockSpec(memory_space=pltpu.VMEM), outs),
        scratch_shapes=scratch,
        name=name,
        compiler_params=pltpu.CompilerParams(vmem_limit_bytes=16 * 1024 * 1024),
    )(*scalars, *remote, *arrays)


def shape_of(shape, dtype=f32):
    return jax.ShapeDtypeStruct(shape, dtype)


def byte_sum(state):
    x = state * 34038481 + 76625530
    pairs = (x & 0x00FF00FF) + ((x >> 8) & 0x00FF00FF)
    total = (pairs + (pairs >> 16)) & 0x7FF
    return (total - 510).astype(f32)


def interleave():
    row = iota((128, 128), 0)
    column = iota((128, 128), 1)
    return (column == 4 * (row & 31) + (row >> 5)).astype(f32).astype(bf16)


def exact_product(x, ones):
    rows = x.shape[0]
    high = x.astype(bf16).astype(f32)
    rest = x - high
    middle = rest.astype(bf16).astype(f32)
    low = rest - middle
    parts = jnp.concatenate([high, middle, low], axis=0).astype(bf16)
    product = jnp.dot(parts, ones, preferred_element_type=f32)
    return product[:rows] + product[rows : 2 * rows] + product[2 * rows :]


def tile_of(x, k):
    return x[:, k * 128 : k * 128 + 128]


def send_halves(out_ref, halves):
    copies = out_ref.shape[0] // 2
    for s in range(2):
        for j in range(copies):
            for k in range(5):
                out_ref[s * copies + j, :, k * 128 : k * 128 + 128] = halves[s][k]


def project(hidden, gain, weights, out_ref):
    squares = jnp.sum(hidden * hidden, axis=1, keepdims=True)
    normed = (hidden * gain).astype(bf16)
    y = lax.dot_general(normed, weights, NT, preferred_element_type=f32)
    first = iota((8, 128), 0) < 4
    few = iota((8, 128), 1) < 16
    spread = jnp.broadcast_to(squares, (8, 128))
    tails = [tile_of(y, 16 + k) for k in range(2)]
    tails = [jnp.where(first, tail, pltpu.roll(tail, 112, 1)) for tail in tails]
    for p in range(8):
        tail = tails[p // 4]
        if p % 4:
            tail = pltpu.roll(tail, 128 - 32 * (p % 4), 1)
        out_ref[p, :, :128] = jnp.where(first, tile_of(y, 2 * p), tile_of(y, 2 * p + 1))
        out_ref[p, :, 128:] = jnp.where(few, tail, spread)


def decode_qkv_kernel(codes_hbm, scale_hbm, gain_hbm, hidden_ref, w_hbm, hid_ref, out_ref,
                      codes_ref, scale_ref, gain_ref, w_ref, code_sems, scale_sem, gain_sem,
                      w_sems):
    chunks = code_sems.shape[0]
    chunk_rows = codes_ref.shape[0] // chunks
    copies = []
    for i in range(chunks):
        rows = pl.ds(i * chunk_rows, chunk_rows)
        copies.append(
            pltpu.make_async_copy(codes_hbm.at[rows], codes_ref.at[rows], code_sems.at[i])
        )
    scale_copy = pltpu.make_async_copy(scale_hbm, scale_ref, scale_sem)
    gain_copy = pltpu.make_async_copy(gain_hbm, gain_ref, gain_sem)
    scale_copy.start()
    for copy in copies:
        copy.start()
    gain_copy.start()
    scale_copy.wait()
    lane = iota((32, 128), 1)
    word = iota((32, 128), 0)
    kept = []
    for tile in range(18):
        if tile * 32 % chunk_rows == 0:
            copies[tile * 32 // chunk_rows].wait()
        codes = codes_ref[tile * 32 : tile * 32 + 32, :]
        window = (codes << 16) | (pltpu.roll(codes, 31, 0) << 8) | pltpu.roll(codes, 30, 0)
        scales = jnp.broadcast_to(scale_ref[tile : tile + 1, :], (32, 128)) * (1.0 / CODE_NORM)
        for r in range(4):
            column = jnp.sum(
                jnp.where(lane == 4 * word + r, scales, 0.0), axis=1, keepdims=True
            )
            values = byte_sum((window >> (8 - 2 * r)) & 0xFFFF) * column
            at = tile * 128 + r * 32
            w_ref[at : at + 32, :] = values.astype(bf16)
        if (tile + 1) * 32 % chunk_rows == 0:
            done = tile * 32 // chunk_rows
            rows = pl.ds(done * 4 * chunk_rows, 4 * chunk_rows)
            kept.append(pltpu.make_async_copy(w_ref.at[rows], w_hbm.at[rows], w_sems.at[done]))
            kept[-1].start()
    hidden = hidden_ref[...].astype(f32)
    hidden = jnp.concatenate([hidden, hidden], axis=0)
    hid_ref[...] = hidden
    gain_copy.wait()
    project(hidden, gain_ref[...], w_ref[...], out_ref)
    for copy in kept:
        copy.wait()


def decode_out_kernel(info_ref, codes_ref, scale_ref, other_ref, w_ref):
    s = info_ref[5]
    lane = iota((32, 128), 1)
    within = lane & 31
    for block in range(16):
        own = block < 8
        rows = slice(block % 8 * 32, block % 8 * 32 + 32)
        across = iota((32, 256), 1) == iota((32, 256), 0) + block % 8 * 32
        scale = scale_ref[...] if own else other_ref[256:257, :]
        scale = jnp.broadcast_to(scale, (32, 256)) * (1.0 / CODE_NORM)
        column = jnp.sum(jnp.where(across, scale, 0.0), axis=1, keepdims=True)
        for group in range(2):
            if own:
                codes = jnp.where(
                    s == 0,
                    codes_ref[rows, group * 128 : group * 128 + 128],
                    codes_ref[rows, group * 128 + 256 : group * 128 + 384],
                )
            else:
                codes = other_ref[rows, group * 128 : group * 128 + 128].astype(jnp.int32)
            second = jnp.where(within < 31, pltpu.roll(codes, 127, 1), pltpu.roll(codes, 31, 1))
            third = jnp.where(within < 30, pltpu.roll(codes, 126, 1), pltpu.roll(codes, 30, 1))
            window = (codes << 16) | (second << 8) | third
            for r in range(4):
                values = byte_sum((window >> (8 - 2 * r)) & 0xFFFF) * column
                at = group * 512 + r * 128
                w_ref[block * 32 : block * 32 + 32, at : at + 128] = values.astype(bf16)


def total_of(ref):
    total = ref[0]
    for j in range(1, ref.shape[0]):
        total = total + ref[j]
    return total


def pass_sum_kernel(in_ref, out_ref):
    total = total_of(in_ref)
    for j in range(out_ref.shape[0]):
        out_ref[j] = total


def merged(in_ref):
    parts = range(in_ref.shape[0])
    stats = [in_ref[j, :, 512:] for j in parts]
    top = functools.reduce(jnp.maximum, stats)
    factors = [jnp.exp(x - top) for x in stats]
    sums = stats[0] * pltpu.roll(factors[0], 4, 1)
    for j in parts[1:]:
        sums = sums + stats[j] * pltpu.roll(factors[j], 4, 1)
    accs = []
    for b in range(4):
        at = slice(b * 128, b * 128 + 128)
        acc = in_ref[0, :, at] * factors[0][:, b : b + 1]
        for j in parts[1:]:
            acc = acc + in_ref[j, :, at] * factors[j][:, b : b + 1]
        accs.append(acc)
    return top, sums, accs


def pass_merge_kernel(in_ref, out_ref):
    top, sums, accs = merged(in_ref)
    lane = iota((8, 128), 1)
    stats = jnp.where(lane < 4, top, jnp.where(lane < 8, sums, 0.0))
    for j in range(out_ref.shape[0]):
        for b in range(4):
            out_ref[j, :, b * 128 : b * 128 + 128] = accs[b]
        out_ref[j, :, 512:] = stats


def attend_kernel(features, earlier, info_ref, in_ref, cos_ref, sin_ref, keys_ref, values_ref,
                  *refs):
    out_ref, k_ref, v_ref, q_ref = refs[2 * earlier :]
    first = iota((8, 128), 0) < 4
    lane = iota((8, 128), 1)
    rms = lax.rsqrt(in_ref[0, :, 144:145] / features + EPSILON)
    tiles = [in_ref[p, :, :128] for p in range(8)]
    for k in range(2):
        tail = in_ref[4 * k, :, 128:]
        for p in range(1, 4):
            part = pltpu.roll(in_ref[4 * k + p, :, 128:], 32 * p, 1)
            tail = jnp.where(lane >> 5 == p, part, tail)
        tail = jnp.where(first, tail, pltpu.roll(tail, 16, 1))
        tiles.append(jnp.where(lane & 31 < 16, tail, pltpu.roll(tail, 4, 0)))
    tiles = [tile * rms for tile in tiles]
    x = exact_product(jnp.concatenate(tiles, axis=0), interleave())
    cos = jnp.concatenate([cos_ref[...]] * 18, axis=0)
    sin = jnp.concatenate([sin_ref[...]] * 18, axis=0)
    turned = x[:72] * cos + pltpu.roll(x[:72], 64, 1) * sin
    turned = turned.astype(bf16).astype(f32)
    q_ref[...] = turned[:64]
    new_key = turned[64:]
    new_value = x[72:].astype(bf16).astype(f32)
    k_ref[...] = new_key
    v_ref[...] = new_value
    new_keys = [refs[2 * u][...] for u in range(earlier)] + [new_key]
    new_values = [refs[2 * u + 1][...] for u in range(earlier)] + [new_value]
    owner = info_ref[4] == 0
    length = keys_ref.shape[1]
    place = iota((16, length), 1)
    halves = [[], []]
    stats = [jnp.zeros((8, 128), f32)] * 2
    for b in range(4):
        query = q_ref[pl.ds(b, 16, stride=4), :]
        scores = lax.dot_general(
            query.astype(bf16), keys_ref[b], NT, preferred_element_type=f32
        ) * SCORE_SCALE
        live = place < info_ref[b]
        top = jnp.max(jnp.where(live, scores, -1e30), axis=1, keepdims=True)
        weights = jnp.where(live, jnp.exp(scores - top), 0.0)
        total = jnp.sum(weights, axis=1, keepdims=True)
        acc = jnp.dot(weights.astype(bf16), values_ref[b], preferred_element_type=f32)
        fresh = [
            jnp.where(
                owner,
                jnp.sum(query * key[b : b + 1, :], axis=1, keepdims=True) * SCORE_SCALE,
                -1e30,
            )
            for key in new_keys
        ]
        peak = functools.reduce(jnp.maximum, fresh, top)
        factor = jnp.exp(top - peak)
        total = total * factor
        acc = acc * factor
        for score, value in zip(fresh, new_values):
            weight = jnp.where(owner, jnp.exp(score - peak), 0.0)
            total = total + weight
            acc = acc + weight * value[b : b + 1, :]
        for s in range(2):
            rows = slice(8 * s, 8 * s + 8)
            halves[s].append(acc[rows])
            stats[s] = jnp.where(lane == b, peak[rows], stats[s])
            stats[s] = jnp.where(lane == 4 + b, total[rows], stats[s])
    send_halves(out_ref, [halves[s] + [stats[s]] for s in range(2)])


def finish_kernel(info_ref, in_ref, w_ref, out_ref, rows_ref):
    _, sums, accs = merged(in_ref)
    for b in range(4):
        attended = (accs[b] / sums[:, 4 + b : 5 + b]).astype(bf16).astype(f32)
        rows_ref[b * 8 : b * 8 + 8, :] = attended
        rows_ref[b * 8 + 32 : b * 8 + 40, :] = attended
    attended = jnp.concatenate(
        [rows_ref[pl.ds(t, 8, stride=8), :] for t in range(8)], axis=0
    ).astype(bf16)
    attended = lax.dot_general(attended, interleave(), NT, preferred_element_type=f32)
    block = iota((8, 128), 1) >> 5
    chunks = []
    for group in range(2):
        for r in range(4):
            chunk = jnp.zeros((8, 128), f32)
            for t in range(4):
                at = (group * 4 + t) * 8
                part = attended[at : at + 8]
                if t != r:
                    part = pltpu.roll(part, (t - r) % 4 * 32, 1)
                chunk = jnp.where(block == t, part, chunk)
            chunks.append(chunk)
    columns = jnp.concatenate(chunks, axis=1).astype(bf16)
    update = lax.dot_general(columns, w_ref[...], NT, preferred_element_type=f32)
    first = iota((8, 128), 0) < 4
    own = jnp.where(first, tile_of(update, 0), tile_of(update, 1))
    other = jnp.where(first, tile_of(update, 2), tile_of(update, 3))
    same = info_ref[5] == 0
    blocks = [jnp.where(same, own, other), jnp.where(same, other, own)]
    copies = out_ref.shape[0] // 2
    for s in range(2):
        for j in range(copies):
            out_ref[s * copies + j] = blocks[s]


def updated(in_ref, hid_ref):
    update = total_of(in_ref)
    turned = pltpu.roll(update, 4, 0)
    first = iota((8, 128), 0) < 4
    update = jnp.concatenate(
        [jnp.where(first, update, turned), jnp.where(first, turned, update)], axis=1
    )
    return (hid_ref[...] + update).astype(bf16)


def next_kernel(in_ref, hid_ref, gain_ref, w_ref, new_ref, out_ref):
    hidden = updated(in_ref, hid_ref).astype(f32)
    new_ref[...] = hidden
    project(hidden, gain_ref[...], w_ref[...], out_ref)


def last_kernel(in_ref, hid_ref, out_ref):
    out_ref[...] = updated(in_ref, hid_ref)[:4]


def exchange(value, axes):
    return lax.all_to_all(value, axes, split_axis=0, concat_axis=0, tiled=True)


def shards(features, hidden_in, norm_gain, qkv_codes, qkv_scale, out_codes, out_scale,
           cache_keys, cache_values, lengths):
    near = lax.axis_size(NEAR)
    far = lax.axis_size(FAR)
    heads = lax.axis_size("head")
    gain = norm_gain.reshape(1, -1)
    batch, block_len = cache_keys.shape[:2]
    keys = cache_keys.reshape(batch, block_len, HEAD_DIM)
    values = cache_values.reshape(batch, block_len, HEAD_DIM)
    place = lax.axis_index(SEQ)
    low = lax.axis_index("z_low")
    info = jnp.concatenate(
        [lengths - place * block_len, jnp.stack([place, low]).astype(jnp.int32)]
    )
    wanted = lax.dynamic_slice_in_dim(out_codes, (1 - low) * 256, 256, axis=1)
    wanted = jnp.concatenate(
        [wanted.astype(f32), jnp.broadcast_to(out_scale[None, :], (8, 256))], axis=0
    )
    other = lax.ppermute(wanted, "z_low", [(0, 1), (1, 0)])

    half_dim = HEAD_DIM // 2
    freqs = jnp.exp(
        -(jnp.arange(half_dim, dtype=f32) * (2.0 / HEAD_DIM)) * math.log(ROPE_BASE)
    )
    steps = jnp.arange(DECODE_STEPS, dtype=jnp.int32)
    positions = lengths[None, :] + steps[:, None]
    angles = positions.astype(f32)[:, :, None] * freqs
    cosines, sines = jnp.cos(angles), jnp.sin(angles)
    cosines = jnp.concatenate([cosines, cosines], axis=-1)
    sines = jnp.concatenate([-sines, sines], axis=-1)
    cosines = tuple(cosines[step] for step in range(DECODE_STEPS))
    sines = tuple(sines[step] for step in range(DECODE_STEPS))

    w_qkv, hidden, partial = call(
        decode_qkv_kernel,
        (pltpu.HBM((2304, 256), bf16), shape_of((8, 256)), shape_of((near, 8, 256))),
        "decode_qkv",
        (hidden_in,),
        remote=(qkv_codes.T, qkv_scale.reshape(18, 128), gain),
        scratch=(
            pltpu.VMEM((576, 256), jnp.int32),
            pltpu.VMEM((18, 128), f32),
            pltpu.VMEM((1, 256), f32),
            pltpu.VMEM((2304, 256), bf16),
            pltpu.SemaphoreType.DMA((6,)),
            pltpu.SemaphoreType.DMA,
            pltpu.SemaphoreType.DMA,
            pltpu.SemaphoreType.DMA((6,)),
        ),
        out_specs=(
            pl.BlockSpec(memory_space=pltpu.HBM),
            pl.BlockSpec(memory_space=pltpu.VMEM),
            pl.BlockSpec(memory_space=pltpu.VMEM),
        ),
    )
    fresh = ()
    for step in range(DECODE_STEPS):
        partial = exchange(partial, NEAR)
        if step == 0:
            partial, other, info, cosines, sines = lax.optimization_barrier(
                (partial, other, info, cosines, sines)
            )
            w_out = call(
                decode_out_kernel,
                shape_of((512, 1024), bf16),
                "decode_out",
                (out_codes, out_scale.reshape(1, -1), other),
                (info,),
            )
        partial = call(pass_sum_kernel, shape_of((far, 8, 256)), "sum_near", (partial,))
        partial = exchange(partial, FAR)
        partial = call(pass_sum_kernel, shape_of((near, 8, 256)), "sum_far", (partial,))
        partial = exchange(partial, NEAR)
        part, new_key, new_value = call(
            functools.partial(attend_kernel, features, step),
            (shape_of((near, 8, 640)), shape_of((8, 128)), shape_of((8, 128))),
            "attend",
            (partial, cosines[step], sines[step], keys, values, *fresh),
            (info,),
            scratch=(pltpu.VMEM((64, 128), f32),),
        )
        fresh += (new_key, new_value)
        part = exchange(part, NEAR)
        part = call(pass_merge_kernel, shape_of((far, 8, 640)), "merge_near", (part,))
        part = exchange(part, FAR)
        update = call(
            finish_kernel,
            shape_of((2 * heads, 8, 128)),
            "finish",
            (part, w_out),
            (info,),
            scratch=(pltpu.VMEM((64, 128), f32),),
        )
        update = exchange(update, ("z_low", "head"))
        if step + 1 < DECODE_STEPS:
            hidden, partial = call(
                next_kernel,
                (shape_of((8, 256)), shape_of((near, 8, 256))),
                "next_step",
                (update, hidden, gain, w_qkv),
            )
    return call(last_kernel, shape_of((4, 256), bf16), "last", (update, hidden))


def solution(mesh):
    seq, head = mesh.shape["seq"], mesh.shape["head"]
    far = seq // 8
    split = Mesh(mesh.devices.reshape(far, 2, 4, head), (*SEQ, "head"))
    placed = (
        P(None, SEQ),
        P(SEQ),
        P(SEQ, "head"),
        P("head"),
        P(SEQ, "head"),
        P(SEQ),
        P(None, SEQ, "head", None),
        P(None, SEQ, "head", None),
        P(),
    )

    def run(hidden_in, *others):
        features = hidden_in.shape[1]
        return jax.shard_map(
            functools.partial(shards, float(features)),
            mesh=split,
            in_specs=placed,
            out_specs=P(None, SEQ),
            check_vma=False,
        )(hidden_in, *others)

    return run
```

```python
import functools
import math

import jax
import jax.numpy as jnp
from jax import lax
from jax.experimental import pallas as pl
from jax.experimental.pallas import tpu as pltpu
from jax.sharding import Mesh
from jax.sharding import PartitionSpec as P

HEAD_DIM = 128
GROUPS = 16
DECODE_STEPS = 2
NEAR = ("z_low", "y")
FAR = "z_high"
SEQ = (FAR, *NEAR)

CODE_NORM = 147.8
EPSILON = 1e-05
ROPE_BASE = 500000.0
SCORE_SCALE = HEAD_DIM ** (-0.5)

f32 = jnp.float32
bf16 = jnp.bfloat16
NT = (((1,), (1,)), ((), ()))


def iota(shape, axis):
    return lax.broadcasted_iota(jnp.int32, shape, axis)


def call(kernel, outs, name, arrays, scalars=(), remote=(), scratch=(), out_specs=None):
    specs = [pl.BlockSpec(memory_space=pltpu.SMEM) for _ in scalars]
    specs += [pl.BlockSpec(memory_space=pltpu.HBM) for _ in remote]
    specs += [pl.BlockSpec(memory_space=pltpu.VMEM) for _ in arrays]
    remote = [pltpu.with_memory_space_constraint(x, pltpu.HBM) for x in remote]
    return pl.pallas_call(
        kernel,
        out_shape=outs,
        in_specs=specs,
        out_specs=out_specs or jax.tree.map(lambda _: pl.BlockSpec(memory_space=pltpu.VMEM), outs),
        scratch_shapes=scratch,
        name=name,
        compiler_params=pltpu.CompilerParams(vmem_limit_bytes=16 * 1024 * 1024),
    )(*scalars, *remote, *arrays)


def shape_of(shape, dtype=f32):
    return jax.ShapeDtypeStruct(shape, dtype)


def byte_sum(state):
    x = state * 34038481 + 76625530
    pairs = (x & 0x00FF00FF) + ((x >> 8) & 0x00FF00FF)
    total = (pairs + (pairs >> 16)) & 0x7FF
    return (total - 510).astype(f32)


def interleave():
    row = iota((128, 128), 0)
    column = iota((128, 128), 1)
    return (column == 4 * (row & 31) + (row >> 5)).astype(f32).astype(bf16)


def exact_product(x, ones):
    rows = x.shape[0]
    high = x.astype(bf16).astype(f32)
    rest = x - high
    middle = rest.astype(bf16).astype(f32)
    low = rest - middle
    parts = jnp.concatenate([high, middle, low], axis=0).astype(bf16)
    product = jnp.dot(parts, ones, preferred_element_type=f32)
    return product[:rows] + product[rows : 2 * rows] + product[2 * rows :]


def tile_of(x, k):
    return x[:, k * 128 : k * 128 + 128]


def send_halves(out_ref, halves):
    copies = out_ref.shape[0] // 2
    for s in range(2):
        for j in range(copies):
            for k in range(5):
                out_ref[s * copies + j, :, k * 128 : k * 128 + 128] = halves[s][k]


def project(hidden, gain, weights, out_ref):
    squares = jnp.sum(hidden * hidden, axis=1, keepdims=True)
    normed = (hidden * gain).astype(bf16)
    y = lax.dot_general(normed, weights, NT, preferred_element_type=f32)
    first = iota((8, 128), 0) < 4
    few = iota((8, 128), 1) < 16
    spread = jnp.broadcast_to(squares, (8, 128))
    tails = [tile_of(y, 16 + k) for k in range(2)]
    tails = [jnp.where(first, tail, pltpu.roll(tail, 112, 1)) for tail in tails]
    for p in range(8):
        tail = tails[p // 4]
        if p % 4:
            tail = pltpu.roll(tail, 128 - 32 * (p % 4), 1)
        out_ref[p, :, :128] = jnp.where(first, tile_of(y, 2 * p), tile_of(y, 2 * p + 1))
        out_ref[p, :, 128:] = jnp.where(few, tail, spread)


def decode_qkv_kernel(codes_hbm, scale_hbm, gain_hbm, hidden_ref, w_hbm, hid_ref, out_ref,
                      codes_ref, scale_ref, gain_ref, w_ref, code_sems, scale_sem, gain_sem,
                      w_sems):
    chunks = code_sems.shape[0]
    chunk_rows = codes_ref.shape[0] // chunks
    copies = []
    for i in range(chunks):
        rows = pl.ds(i * chunk_rows, chunk_rows)
        copies.append(
            pltpu.make_async_copy(codes_hbm.at[rows], codes_ref.at[rows], code_sems.at[i])
        )
    scale_copy = pltpu.make_async_copy(scale_hbm, scale_ref, scale_sem)
    gain_copy = pltpu.make_async_copy(gain_hbm, gain_ref, gain_sem)
    scale_copy.start()
    for copy in copies:
        copy.start()
    gain_copy.start()
    scale_copy.wait()
    lane = iota((32, 128), 1)
    word = iota((32, 128), 0)
    kept = []
    for tile in range(18):
        if tile * 32 % chunk_rows == 0:
            copies[tile * 32 // chunk_rows].wait()
        codes = codes_ref[tile * 32 : tile * 32 + 32, :]
        window = (codes << 16) | (pltpu.roll(codes, 31, 0) << 8) | pltpu.roll(codes, 30, 0)
        scales = jnp.broadcast_to(scale_ref[tile : tile + 1, :], (32, 128)) * (1.0 / CODE_NORM)
        for r in range(4):
            column = jnp.sum(
                jnp.where(lane == 4 * word + r, scales, 0.0), axis=1, keepdims=True
            )
            values = byte_sum((window >> (8 - 2 * r)) & 0xFFFF) * column
            at = tile * 128 + r * 32
            w_ref[at : at + 32, :] = values.astype(bf16)
        if (tile + 1) * 32 % chunk_rows == 0:
            done = tile * 32 // chunk_rows
            rows = pl.ds(done * 4 * chunk_rows, 4 * chunk_rows)
            kept.append(pltpu.make_async_copy(w_ref.at[rows], w_hbm.at[rows], w_sems.at[done]))
            kept[-1].start()
    hidden = hidden_ref[...].astype(f32)
    hidden = jnp.concatenate([hidden, hidden], axis=0)
    hid_ref[...] = hidden
    gain_copy.wait()
    project(hidden, gain_ref[...], w_ref[...], out_ref)
    for copy in kept:
        copy.wait()


def decode_out_kernel(info_ref, codes_ref, scale_ref, other_ref, w_ref):
    s = info_ref[5]
    lane = iota((32, 128), 1)
    within = lane & 31
    for block in range(16):
        own = block < 8
        rows = slice(block % 8 * 32, block % 8 * 32 + 32)
        across = iota((32, 256), 1) == iota((32, 256), 0) + block % 8 * 32
        scale = scale_ref[...] if own else other_ref[256:257, :]
        scale = jnp.broadcast_to(scale, (32, 256)) * (1.0 / CODE_NORM)
        column = jnp.sum(jnp.where(across, scale, 0.0), axis=1, keepdims=True)
        for group in range(2):
            if own:
                codes = jnp.where(
                    s == 0,
                    codes_ref[rows, group * 128 : group * 128 + 128],
                    codes_ref[rows, group * 128 + 256 : group * 128 + 384],
                )
            else:
                codes = other_ref[rows, group * 128 : group * 128 + 128].astype(jnp.int32)
            second = jnp.where(within < 31, pltpu.roll(codes, 127, 1), pltpu.roll(codes, 31, 1))
            third = jnp.where(within < 30, pltpu.roll(codes, 126, 1), pltpu.roll(codes, 30, 1))
            window = (codes << 16) | (second << 8) | third
            for r in range(4):
                values = byte_sum((window >> (8 - 2 * r)) & 0xFFFF) * column
                at = group * 512 + r * 128
                w_ref[block * 32 : block * 32 + 32, at : at + 128] = values.astype(bf16)


def total_of(ref):
    total = ref[0]
    for j in range(1, ref.shape[0]):
        total = total + ref[j]
    return total


def pass_sum_kernel(in_ref, out_ref):
    total = total_of(in_ref)
    for j in range(out_ref.shape[0]):
        out_ref[j] = total


def merged(in_ref):
    parts = range(in_ref.shape[0])
    stats = [in_ref[j, :, 512:] for j in parts]
    top = functools.reduce(jnp.maximum, stats)
    factors = [jnp.exp(x - top) for x in stats]
    sums = stats[0] * pltpu.roll(factors[0], 4, 1)
    for j in parts[1:]:
        sums = sums + stats[j] * pltpu.roll(factors[j], 4, 1)
    accs = []
    for b in range(4):
        at = slice(b * 128, b * 128 + 128)
        acc = in_ref[0, :, at] * factors[0][:, b : b + 1]
        for j in parts[1:]:
            acc = acc + in_ref[j, :, at] * factors[j][:, b : b + 1]
        accs.append(acc)
    return top, sums, accs


def pass_merge_kernel(in_ref, out_ref):
    top, sums, accs = merged(in_ref)
    lane = iota((8, 128), 1)
    stats = jnp.where(lane < 4, top, jnp.where(lane < 8, sums, 0.0))
    for j in range(out_ref.shape[0]):
        for b in range(4):
            out_ref[j, :, b * 128 : b * 128 + 128] = accs[b]
        out_ref[j, :, 512:] = stats


def attend_kernel(features, earlier, info_ref, in_ref, cos_ref, sin_ref, keys_ref, values_ref,
                  *refs):
    out_ref, k_ref, v_ref, q_ref = refs[2 * earlier :]
    first = iota((8, 128), 0) < 4
    lane = iota((8, 128), 1)
    rms = lax.rsqrt(in_ref[0, :, 144:145] / features + EPSILON)
    tiles = [in_ref[p, :, :128] for p in range(8)]
    for k in range(2):
        tail = in_ref[4 * k, :, 128:]
        for p in range(1, 4):
            part = pltpu.roll(in_ref[4 * k + p, :, 128:], 32 * p, 1)
            tail = jnp.where(lane >> 5 == p, part, tail)
        tail = jnp.where(first, tail, pltpu.roll(tail, 16, 1))
        tiles.append(jnp.where(lane & 31 < 16, tail, pltpu.roll(tail, 4, 0)))
    tiles = [tile * rms for tile in tiles]
    x = exact_product(jnp.concatenate(tiles, axis=0), interleave())
    cos = jnp.concatenate([cos_ref[...]] * 18, axis=0)
    sin = jnp.concatenate([sin_ref[...]] * 18, axis=0)
    turned = x[:72] * cos + pltpu.roll(x[:72], 64, 1) * sin
    turned = turned.astype(bf16).astype(f32)
    q_ref[...] = turned[:64]
    new_key = turned[64:]
    new_value = x[72:].astype(bf16).astype(f32)
    k_ref[...] = new_key
    v_ref[...] = new_value
    new_keys = [refs[2 * u][...] for u in range(earlier)] + [new_key]
    new_values = [refs[2 * u + 1][...] for u in range(earlier)] + [new_value]
    owner = info_ref[4] == 0
    length = keys_ref.shape[1]
    place = iota((16, length), 1)
    halves = [[], []]
    stats = [jnp.zeros((8, 128), f32)] * 2
    tops, totals, pair_accs = [], [], []
    for pair in (0, 2):
        queries = [q_ref[pl.ds(b, 16, stride=4), :] for b in (pair, pair + 1)]
        empty = jnp.zeros((16, 128), f32)
        both = jnp.concatenate(
            [
                jnp.concatenate([queries[0], empty], axis=1),
                jnp.concatenate([empty, queries[1]], axis=1),
            ],
            axis=0,
        ).astype(bf16)
        keys = jnp.concatenate([keys_ref[pair], keys_ref[pair + 1]], axis=1)
        values = jnp.concatenate([values_ref[pair], values_ref[pair + 1]], axis=1)
        scores = lax.dot_general(both, keys, NT, preferred_element_type=f32) * SCORE_SCALE
        rounded = []
        for k in range(2):
            score = scores[16 * k : 16 * k + 16]
            live = place < info_ref[pair + k]
            top = jnp.max(jnp.where(live, score, -1e30), axis=1, keepdims=True)
            weights = jnp.where(live, jnp.exp(score - top), 0.0)
            tops.append(top)
            totals.append(jnp.sum(weights, axis=1, keepdims=True))
            rounded.append(weights.astype(bf16))
        acc = jnp.dot(
            jnp.concatenate(rounded, axis=0), values, preferred_element_type=f32
        )
        pair_accs += [acc[:16, :128], acc[16:, 128:]]
    for b in range(4):
        query = q_ref[pl.ds(b, 16, stride=4), :]
        top, total, acc = tops[b], totals[b], pair_accs[b]
        fresh = [
            jnp.where(
                owner,
                jnp.sum(query * key[b : b + 1, :], axis=1, keepdims=True) * SCORE_SCALE,
                -1e30,
            )
            for key in new_keys
        ]
        peak = functools.reduce(jnp.maximum, fresh, top)
        factor = jnp.exp(top - peak)
        total = total * factor
        acc = acc * factor
        for score, value in zip(fresh, new_values):
            weight = jnp.where(owner, jnp.exp(score - peak), 0.0)
            total = total + weight
            acc = acc + weight * value[b : b + 1, :]
        for s in range(2):
            rows = slice(8 * s, 8 * s + 8)
            halves[s].append(acc[rows])
            stats[s] = jnp.where(lane == b, peak[rows], stats[s])
            stats[s] = jnp.where(lane == 4 + b, total[rows], stats[s])
    send_halves(out_ref, [halves[s] + [stats[s]] for s in range(2)])


def finish_kernel(info_ref, in_ref, w_ref, out_ref, rows_ref):
    _, sums, accs = merged(in_ref)
    for b in range(4):
        attended = (accs[b] / sums[:, 4 + b : 5 + b]).astype(bf16).astype(f32)
        rows_ref[b * 8 : b * 8 + 8, :] = attended
        rows_ref[b * 8 + 32 : b * 8 + 40, :] = attended
    attended = jnp.concatenate(
        [rows_ref[pl.ds(t, 8, stride=8), :] for t in range(8)], axis=0
    ).astype(bf16)
    attended = lax.dot_general(attended, interleave(), NT, preferred_element_type=f32)
    block = iota((8, 128), 1) >> 5
    chunks = []
    for group in range(2):
        for r in range(4):
            chunk = jnp.zeros((8, 128), f32)
            for t in range(4):
                at = (group * 4 + t) * 8
                part = attended[at : at + 8]
                if t != r:
                    part = pltpu.roll(part, (t - r) % 4 * 32, 1)
                chunk = jnp.where(block == t, part, chunk)
            chunks.append(chunk)
    columns = jnp.concatenate(chunks, axis=1).astype(bf16)
    update = lax.dot_general(columns, w_ref[...], NT, preferred_element_type=f32)
    first = iota((8, 128), 0) < 4
    own = jnp.where(first, tile_of(update, 0), tile_of(update, 1))
    other = jnp.where(first, tile_of(update, 2), tile_of(update, 3))
    same = info_ref[5] == 0
    blocks = [jnp.where(same, own, other), jnp.where(same, other, own)]
    copies = out_ref.shape[0] // 2
    for s in range(2):
        for j in range(copies):
            out_ref[s * copies + j] = blocks[s]


def updated(in_ref, hid_ref):
    update = total_of(in_ref)
    turned = pltpu.roll(update, 4, 0)
    first = iota((8, 128), 0) < 4
    update = jnp.concatenate(
        [jnp.where(first, update, turned), jnp.where(first, turned, update)], axis=1
    )
    return (hid_ref[...] + update).astype(bf16)


def next_kernel(in_ref, hid_ref, gain_ref, w_ref, new_ref, out_ref):
    hidden = updated(in_ref, hid_ref).astype(f32)
    new_ref[...] = hidden
    project(hidden, gain_ref[...], w_ref[...], out_ref)


def last_kernel(in_ref, hid_ref, out_ref):
    out_ref[...] = updated(in_ref, hid_ref)[:4]


def exchange(value, axes):
    return lax.all_to_all(value, axes, split_axis=0, concat_axis=0, tiled=True)


def shards(features, hidden_in, norm_gain, qkv_codes, qkv_scale, out_codes, out_scale,
           cache_keys, cache_values, lengths):
    near = lax.axis_size(NEAR)
    far = lax.axis_size(FAR)
    heads = lax.axis_size("head")
    gain = norm_gain.reshape(1, -1)
    batch, block_len = cache_keys.shape[:2]
    keys = cache_keys.reshape(batch, block_len, HEAD_DIM)
    values = cache_values.reshape(batch, block_len, HEAD_DIM)
    place = lax.axis_index(SEQ)
    low = lax.axis_index("z_low")
    info = jnp.concatenate(
        [lengths - place * block_len, jnp.stack([place, low]).astype(jnp.int32)]
    )
    wanted = lax.dynamic_slice_in_dim(out_codes, (1 - low) * 256, 256, axis=1)
    wanted = jnp.concatenate(
        [wanted.astype(f32), jnp.broadcast_to(out_scale[None, :], (8, 256))], axis=0
    )

    half_dim = HEAD_DIM // 2
    freqs = jnp.exp(
        -(jnp.arange(half_dim, dtype=f32) * (2.0 / HEAD_DIM)) * math.log(ROPE_BASE)
    )
    steps = jnp.arange(DECODE_STEPS, dtype=jnp.int32)
    positions = lengths[None, :] + steps[:, None]
    angles = positions.astype(f32)[:, :, None] * freqs
    cosines, sines = jnp.cos(angles), jnp.sin(angles)
    cosines = jnp.concatenate([cosines, cosines], axis=-1)
    sines = jnp.concatenate([-sines, sines], axis=-1)
    cosines = tuple(cosines[step] for step in range(DECODE_STEPS))
    sines = tuple(sines[step] for step in range(DECODE_STEPS))

    w_qkv, hidden, partial = call(
        decode_qkv_kernel,
        (pltpu.HBM((2304, 256), bf16), shape_of((8, 256)), shape_of((near, 8, 256))),
        "decode_qkv",
        (hidden_in,),
        remote=(qkv_codes.T, qkv_scale.reshape(18, 128), gain),
        scratch=(
            pltpu.VMEM((576, 256), jnp.int32),
            pltpu.VMEM((18, 128), f32),
            pltpu.VMEM((1, 256), f32),
            pltpu.VMEM((2304, 256), bf16),
            pltpu.SemaphoreType.DMA((6,)),
            pltpu.SemaphoreType.DMA,
            pltpu.SemaphoreType.DMA,
            pltpu.SemaphoreType.DMA((6,)),
        ),
        out_specs=(
            pl.BlockSpec(memory_space=pltpu.HBM),
            pl.BlockSpec(memory_space=pltpu.VMEM),
            pl.BlockSpec(memory_space=pltpu.VMEM),
        ),
    )
    fresh = ()
    for step in range(DECODE_STEPS):
        partial = exchange(partial, NEAR)
        if step == 0:
            partial, wanted, info, cosines, sines = lax.optimization_barrier(
                (partial, wanted, info, cosines, sines)
            )
            other = lax.ppermute(wanted, "z_low", [(0, 1), (1, 0)])
        partial = call(pass_sum_kernel, shape_of((far, 8, 256)), "sum_near", (partial,))
        partial = exchange(partial, FAR)
        partial = call(pass_sum_kernel, shape_of((near, 8, 256)), "sum_far", (partial,))
        partial = exchange(partial, NEAR)
        if step == 0:
            partial, other = lax.optimization_barrier((partial, other))
        part, new_key, new_value = call(
            functools.partial(attend_kernel, features, step),
            (shape_of((near, 8, 640)), shape_of((8, 128)), shape_of((8, 128))),
            "attend",
            (partial, cosines[step], sines[step], keys, values, *fresh),
            (info,),
            scratch=(pltpu.VMEM((64, 128), f32),),
        )
        fresh += (new_key, new_value)
        part = exchange(part, NEAR)
        if step == 0:
            w_out = call(
                decode_out_kernel,
                shape_of((512, 1024), bf16),
                "decode_out",
                (out_codes, out_scale.reshape(1, -1), other),
                (info,),
            )
        part = call(pass_merge_kernel, shape_of((far, 8, 640)), "merge_near", (part,))
        part = exchange(part, FAR)
        update = call(
            finish_kernel,
            shape_of((2 * heads, 8, 128)),
            "finish",
            (part, w_out),
            (info,),
            scratch=(pltpu.VMEM((64, 128), f32),),
        )
        update = exchange(update, ("z_low", "head"))
        if step + 1 < DECODE_STEPS:
            hidden, partial = call(
                next_kernel,
                (shape_of((8, 256)), shape_of((near, 8, 256))),
                "next_step",
                (update, hidden, gain, w_qkv),
            )
    return call(last_kernel, shape_of((4, 256), bf16), "last", (update, hidden))


def solution(mesh):
    seq, head = mesh.shape["seq"], mesh.shape["head"]
    far = seq // 8
    split = Mesh(mesh.devices.reshape(far, 2, 4, head), (*SEQ, "head"))
    placed = (
        P(None, SEQ),
        P(SEQ),
        P(SEQ, "head"),
        P("head"),
        P(SEQ, "head"),
        P(SEQ),
        P(None, SEQ, "head", None),
        P(None, SEQ, "head", None),
        P(),
    )

    def run(hidden_in, *others):
        features = hidden_in.shape[1]
        return jax.shard_map(
            functools.partial(shards, float(features)),
            mesh=split,
            in_specs=placed,
            out_specs=P(None, SEQ),
            check_vma=False,
        )(hidden_in, *others)

    return run
```

```python
import functools
import math

import jax
import jax.numpy as jnp
from jax import lax
from jax.experimental import pallas as pl
from jax.experimental.pallas import tpu as pltpu
from jax.sharding import Mesh
from jax.sharding import PartitionSpec as P

HEAD_DIM = 128
GROUPS = 16
DECODE_STEPS = 2
NEAR = ("z_low", "y")
FAR = "z_high"
SEQ = (FAR, *NEAR)

CODE_NORM = 147.8
EPSILON = 1e-05
ROPE_BASE = 500000.0
SCORE_SCALE = HEAD_DIM ** (-0.5)

f32 = jnp.float32
bf16 = jnp.bfloat16
NT = (((1,), (1,)), ((), ()))


def iota(shape, axis):
    return lax.broadcasted_iota(jnp.int32, shape, axis)


def call(kernel, outs, name, arrays, scalars=(), remote=(), scratch=(), out_specs=None):
    specs = [pl.BlockSpec(memory_space=pltpu.SMEM) for _ in scalars]
    specs += [pl.BlockSpec(memory_space=pltpu.HBM) for _ in remote]
    specs += [pl.BlockSpec(memory_space=pltpu.VMEM) for _ in arrays]
    remote = [pltpu.with_memory_space_constraint(x, pltpu.HBM) for x in remote]
    return pl.pallas_call(
        kernel,
        out_shape=outs,
        in_specs=specs,
        out_specs=out_specs or jax.tree.map(lambda _: pl.BlockSpec(memory_space=pltpu.VMEM), outs),
        scratch_shapes=scratch,
        name=name,
        compiler_params=pltpu.CompilerParams(vmem_limit_bytes=16 * 1024 * 1024),
    )(*scalars, *remote, *arrays)


def shape_of(shape, dtype=f32):
    return jax.ShapeDtypeStruct(shape, dtype)


def byte_sum(state):
    x = state * 34038481 + 76625530
    pairs = (x & 0x00FF00FF) + ((x >> 8) & 0x00FF00FF)
    total = (pairs + (pairs >> 16)) & 0x7FF
    return (total - 510).astype(f32)


def interleave():
    row = iota((128, 128), 0)
    column = iota((128, 128), 1)
    return (column == 4 * (row & 31) + (row >> 5)).astype(f32).astype(bf16)


def exact_product(x, ones):
    rows = x.shape[0]
    high = x.astype(bf16).astype(f32)
    rest = x - high
    middle = rest.astype(bf16).astype(f32)
    low = rest - middle
    parts = jnp.concatenate([high, middle, low], axis=0).astype(bf16)
    product = jnp.dot(parts, ones, preferred_element_type=f32)
    return product[:rows] + product[rows : 2 * rows] + product[2 * rows :]


def tile_of(x, k):
    return x[:, k * 128 : k * 128 + 128]


def send_halves(out_ref, halves):
    copies = out_ref.shape[0] // 2
    for s in range(2):
        for j in range(copies):
            for k in range(5):
                out_ref[s * copies + j, :, k * 128 : k * 128 + 128] = halves[s][k]


def norm(hidden, gain):
    squares = jnp.sum(hidden * hidden, axis=1, keepdims=True)
    return (hidden * gain).astype(bf16), squares


def pack(y, squares, out_ref):
    first = iota((8, 128), 0) < 4
    few = iota((8, 128), 1) < 16
    spread = jnp.broadcast_to(squares, (8, 128))
    tails = [tile_of(y, 16 + k) for k in range(2)]
    tails = [jnp.where(first, tail, pltpu.roll(tail, 112, 1)) for tail in tails]
    for p in range(8):
        tail = tails[p // 4]
        if p % 4:
            tail = pltpu.roll(tail, 128 - 32 * (p % 4), 1)
        out_ref[p, :, :128] = jnp.where(first, tile_of(y, 2 * p), tile_of(y, 2 * p + 1))
        out_ref[p, :, 128:] = jnp.where(few, tail, spread)


def decode_qkv_kernel(codes_hbm, scale_hbm, gain_hbm, hidden_ref, w_hbm, hid_ref, out_ref,
                      codes_ref, scale_ref, gain_ref, w_ref, code_sems, scale_sem, gain_sem,
                      w_sems):
    chunks = code_sems.shape[0]
    chunk_rows = codes_ref.shape[0] // chunks
    copies = []
    for i in range(chunks):
        rows = pl.ds(i * chunk_rows, chunk_rows)
        copies.append(
            pltpu.make_async_copy(codes_hbm.at[rows], codes_ref.at[rows], code_sems.at[i])
        )
    scale_copy = pltpu.make_async_copy(scale_hbm, scale_ref, scale_sem)
    gain_copy = pltpu.make_async_copy(gain_hbm, gain_ref, gain_sem)
    scale_copy.start()
    gain_copy.start()
    for copy in copies:
        copy.start()
    hidden = hidden_ref[...].astype(f32)
    hidden = jnp.concatenate([hidden, hidden], axis=0)
    hid_ref[...] = hidden
    scale_copy.wait()
    gain_copy.wait()
    normed, squares = norm(hidden, gain_ref[...])
    lane = iota((32, 128), 1)
    word = iota((32, 128), 0)
    kept, products = [], []
    for tile in range(18):
        if tile * 32 % chunk_rows == 0:
            copies[tile * 32 // chunk_rows].wait()
        codes = codes_ref[tile * 32 : tile * 32 + 32, :]
        window = (codes << 16) | (pltpu.roll(codes, 31, 0) << 8) | pltpu.roll(codes, 30, 0)
        scales = jnp.broadcast_to(scale_ref[tile : tile + 1, :], (32, 128)) * (1.0 / CODE_NORM)
        for r in range(4):
            column = jnp.sum(
                jnp.where(lane == 4 * word + r, scales, 0.0), axis=1, keepdims=True
            )
            values = byte_sum((window >> (8 - 2 * r)) & 0xFFFF) * column
            at = tile * 128 + r * 32
            w_ref[at : at + 32, :] = values.astype(bf16)
        if (tile + 1) * 32 % chunk_rows == 0:
            done = tile * 32 // chunk_rows
            rows = pl.ds(done * 4 * chunk_rows, 4 * chunk_rows)
            kept.append(pltpu.make_async_copy(w_ref.at[rows], w_hbm.at[rows], w_sems.at[done]))
            kept[-1].start()
            products.append(
                lax.dot_general(normed, w_ref[rows, :], NT, preferred_element_type=f32)
            )
    pack(jnp.concatenate(products, axis=1), squares, out_ref)
    for copy in kept:
        copy.wait()


def decode_out_kernel(info_ref, codes_ref, scale_ref, other_ref, w_ref):
    s = info_ref[5]
    lane = iota((32, 128), 1)
    within = lane & 31
    for block in range(16):
        own = block < 8
        rows = slice(block % 8 * 32, block % 8 * 32 + 32)
        across = iota((32, 256), 1) == iota((32, 256), 0) + block % 8 * 32
        scale = scale_ref[...] if own else other_ref[256:257, :]
        scale = jnp.broadcast_to(scale, (32, 256)) * (1.0 / CODE_NORM)
        column = jnp.sum(jnp.where(across, scale, 0.0), axis=1, keepdims=True)
        for group in range(2):
            if own:
                codes = jnp.where(
                    s == 0,
                    codes_ref[rows, group * 128 : group * 128 + 128],
                    codes_ref[rows, group * 128 + 256 : group * 128 + 384],
                )
            else:
                codes = other_ref[rows, group * 128 : group * 128 + 128].astype(jnp.int32)
            second = jnp.where(within < 31, pltpu.roll(codes, 127, 1), pltpu.roll(codes, 31, 1))
            third = jnp.where(within < 30, pltpu.roll(codes, 126, 1), pltpu.roll(codes, 30, 1))
            window = (codes << 16) | (second << 8) | third
            for r in range(4):
                values = byte_sum((window >> (8 - 2 * r)) & 0xFFFF) * column
                at = group * 512 + r * 128
                w_ref[block * 32 : block * 32 + 32, at : at + 128] = values.astype(bf16)


def total_of(ref):
    total = ref[0]
    for j in range(1, ref.shape[0]):
        total = total + ref[j]
    return total


def pass_sum_kernel(in_ref, out_ref):
    total = total_of(in_ref)
    for j in range(out_ref.shape[0]):
        out_ref[j] = total


def merged(in_ref):
    parts = range(in_ref.shape[0])
    stats = [in_ref[j, :, 512:] for j in parts]
    top = functools.reduce(jnp.maximum, stats)
    factors = [jnp.exp(x - top) for x in stats]
    sums = stats[0] * pltpu.roll(factors[0], 4, 1)
    for j in parts[1:]:
        sums = sums + stats[j] * pltpu.roll(factors[j], 4, 1)
    accs = []
    for b in range(4):
        at = slice(b * 128, b * 128 + 128)
        acc = in_ref[0, :, at] * factors[0][:, b : b + 1]
        for j in parts[1:]:
            acc = acc + in_ref[j, :, at] * factors[j][:, b : b + 1]
        accs.append(acc)
    return top, sums, accs


def pass_merge_kernel(in_ref, out_ref):
    top, sums, accs = merged(in_ref)
    lane = iota((8, 128), 1)
    stats = jnp.where(lane < 4, top, jnp.where(lane < 8, sums, 0.0))
    for j in range(out_ref.shape[0]):
        for b in range(4):
            out_ref[j, :, b * 128 : b * 128 + 128] = accs[b]
        out_ref[j, :, 512:] = stats


def attend_kernel(features, earlier, info_ref, in_ref, cos_ref, sin_ref, keys_ref, values_ref,
                  *refs):
    out_ref, k_ref, v_ref, q_ref = refs[2 * earlier :]
    first = iota((8, 128), 0) < 4
    lane = iota((8, 128), 1)
    rms = lax.rsqrt(in_ref[0, :, 144:145] / features + EPSILON)
    tiles = [in_ref[p, :, :128] for p in range(8)]
    for k in range(2):
        tail = in_ref[4 * k, :, 128:]
        for p in range(1, 4):
            part = pltpu.roll(in_ref[4 * k + p, :, 128:], 32 * p, 1)
            tail = jnp.where(lane >> 5 == p, part, tail)
        tail = jnp.where(first, tail, pltpu.roll(tail, 16, 1))
        tiles.append(jnp.where(lane & 31 < 16, tail, pltpu.roll(tail, 4, 0)))
    tiles = [tile * rms for tile in tiles]
    x = exact_product(jnp.concatenate(tiles, axis=0), interleave())
    cos = jnp.concatenate([cos_ref[...]] * 18, axis=0)
    sin = jnp.concatenate([sin_ref[...]] * 18, axis=0)
    turned = x[:72] * cos + pltpu.roll(x[:72], 64, 1) * sin
    turned = turned.astype(bf16).astype(f32)
    q_ref[...] = turned[:64]
    new_key = turned[64:]
    new_value = x[72:].astype(bf16).astype(f32)
    k_ref[...] = new_key
    v_ref[...] = new_value
    new_keys = [refs[2 * u][...] for u in range(earlier)] + [new_key]
    new_values = [refs[2 * u + 1][...] for u in range(earlier)] + [new_value]
    owner = info_ref[4] == 0

    def by_head(rows):
        return jnp.concatenate(
            [jnp.broadcast_to(rows[b : b + 1, :], (16, 128)) for b in range(4)], axis=0
        )

    by_sequence = [q_ref[pl.ds(b, 16, stride=4), :] for b in range(4)]
    queries = jnp.concatenate(by_sequence, axis=0)
    fresh = [
        jnp.where(
            owner,
            jnp.sum(queries * by_head(key), axis=1, keepdims=True) * SCORE_SCALE,
            -1e30,
        )
        for key in new_keys
    ]
    length = keys_ref.shape[1]
    place = iota((16, length), 1)
    halves = [[], []]
    stats = [jnp.zeros((8, 128), f32)] * 2
    tops, totals, pair_accs = [], [], []
    for pair in (0, 2):
        empty = jnp.zeros((16, 128), f32)
        both = jnp.concatenate(
            [
                jnp.concatenate([by_sequence[pair], empty], axis=1),
                jnp.concatenate([empty, by_sequence[pair + 1]], axis=1),
            ],
            axis=0,
        ).astype(bf16)
        keys = jnp.concatenate([keys_ref[pair], keys_ref[pair + 1]], axis=1)
        values = jnp.concatenate([values_ref[pair], values_ref[pair + 1]], axis=1)
        scores = lax.dot_general(both, keys, NT, preferred_element_type=f32) * SCORE_SCALE
        rounded = []
        for k in range(2):
            score = scores[16 * k : 16 * k + 16]
            live = place < info_ref[pair + k]
            top = jnp.max(jnp.where(live, score, -1e30), axis=1, keepdims=True)
            weights = jnp.where(live, jnp.exp(score - top), 0.0)
            tops.append(top)
            totals.append(jnp.sum(weights, axis=1, keepdims=True))
            rounded.append(weights.astype(bf16))
        acc = jnp.dot(
            jnp.concatenate(rounded, axis=0), values, preferred_element_type=f32
        )
        pair_accs += [acc[:16, :128], acc[16:, 128:]]
    top = jnp.concatenate(tops, axis=0)
    peak = functools.reduce(jnp.maximum, fresh, top)
    factor = jnp.exp(top - peak)
    total = jnp.concatenate(totals, axis=0) * factor
    acc = jnp.concatenate(pair_accs, axis=0) * factor
    for score, value in zip(fresh, new_values):
        weight = jnp.where(owner, jnp.exp(score - peak), 0.0)
        total = total + weight
        acc = acc + weight * by_head(value)
    for b in range(4):
        for s in range(2):
            at = b * 16 + 8 * s
            rows = slice(at, at + 8)
            halves[s].append(acc[rows])
            stats[s] = jnp.where(lane == b, peak[rows], stats[s])
            stats[s] = jnp.where(lane == 4 + b, total[rows], stats[s])
    send_halves(out_ref, [halves[s] + [stats[s]] for s in range(2)])


def finish_kernel(info_ref, in_ref, w_ref, out_ref, rows_ref):
    _, sums, accs = merged(in_ref)
    for b in range(4):
        attended = (accs[b] / sums[:, 4 + b : 5 + b]).astype(bf16).astype(f32)
        rows_ref[b * 8 : b * 8 + 8, :] = attended
        rows_ref[b * 8 + 32 : b * 8 + 40, :] = attended
    attended = jnp.concatenate(
        [rows_ref[pl.ds(t, 8, stride=8), :] for t in range(8)], axis=0
    ).astype(bf16)
    attended = lax.dot_general(attended, interleave(), NT, preferred_element_type=f32)
    block = iota((8, 128), 1) >> 5
    chunks = []
    for group in range(2):
        for r in range(4):
            chunk = jnp.zeros((8, 128), f32)
            for t in range(4):
                at = (group * 4 + t) * 8
                part = attended[at : at + 8]
                if t != r:
                    part = pltpu.roll(part, (t - r) % 4 * 32, 1)
                chunk = jnp.where(block == t, part, chunk)
            chunks.append(chunk)
    columns = jnp.concatenate(chunks, axis=1).astype(bf16)
    update = lax.dot_general(columns, w_ref[...], NT, preferred_element_type=f32)
    first = iota((8, 128), 0) < 4
    own = jnp.where(first, tile_of(update, 0), tile_of(update, 1))
    other = jnp.where(first, tile_of(update, 2), tile_of(update, 3))
    same = info_ref[5] == 0
    blocks = [jnp.where(same, own, other), jnp.where(same, other, own)]
    copies = out_ref.shape[0] // 2
    for s in range(2):
        for j in range(copies):
            out_ref[s * copies + j] = blocks[s]


def updated(in_ref, hid_ref):
    update = total_of(in_ref)
    turned = pltpu.roll(update, 4, 0)
    first = iota((8, 128), 0) < 4
    update = jnp.concatenate(
        [jnp.where(first, update, turned), jnp.where(first, turned, update)], axis=1
    )
    return (hid_ref[...] + update).astype(bf16)


def next_kernel(in_ref, hid_ref, gain_ref, w_ref, new_ref, out_ref):
    hidden = updated(in_ref, hid_ref).astype(f32)
    new_ref[...] = hidden
    normed, squares = norm(hidden, gain_ref[...])
    pack(lax.dot_general(normed, w_ref[...], NT, preferred_element_type=f32), squares, out_ref)


def last_kernel(in_ref, hid_ref, out_ref):
    out_ref[...] = updated(in_ref, hid_ref)[:4]


def exchange(value, axes):
    return lax.all_to_all(value, axes, split_axis=0, concat_axis=0, tiled=True)


def shards(features, hidden_in, norm_gain, qkv_codes, qkv_scale, out_codes, out_scale,
           cache_keys, cache_values, lengths):
    near = lax.axis_size(NEAR)
    far = lax.axis_size(FAR)
    heads = lax.axis_size("head")
    gain = norm_gain.reshape(1, -1)
    batch, block_len = cache_keys.shape[:2]
    keys = cache_keys.reshape(batch, block_len, HEAD_DIM)
    values = cache_values.reshape(batch, block_len, HEAD_DIM)
    place = lax.axis_index(SEQ)
    low = lax.axis_index("z_low")
    info = jnp.concatenate(
        [lengths - place * block_len, jnp.stack([place, low]).astype(jnp.int32)]
    )
    wanted = lax.dynamic_slice_in_dim(out_codes, (1 - low) * 256, 256, axis=1)
    wanted = jnp.concatenate(
        [wanted.astype(f32), jnp.broadcast_to(out_scale[None, :], (8, 256))], axis=0
    )

    half_dim = HEAD_DIM // 2
    freqs = jnp.exp(
        -(jnp.arange(half_dim, dtype=f32) * (2.0 / HEAD_DIM)) * math.log(ROPE_BASE)
    )
    steps = jnp.arange(DECODE_STEPS, dtype=jnp.int32)
    positions = lengths[None, :] + steps[:, None]
    angles = positions.astype(f32)[:, :, None] * freqs
    cosines, sines = jnp.cos(angles), jnp.sin(angles)
    cosines = jnp.concatenate([cosines, cosines], axis=-1)
    sines = jnp.concatenate([-sines, sines], axis=-1)
    cosines = tuple(cosines[step] for step in range(DECODE_STEPS))
    sines = tuple(sines[step] for step in range(DECODE_STEPS))

    w_qkv, hidden, partial = call(
        decode_qkv_kernel,
        (pltpu.HBM((2304, 256), bf16), shape_of((8, 256)), shape_of((near, 8, 256))),
        "decode_qkv",
        (hidden_in,),
        remote=(qkv_codes.T, qkv_scale.reshape(18, 128), gain),
        scratch=(
            pltpu.VMEM((576, 256), jnp.int32),
            pltpu.VMEM((18, 128), f32),
            pltpu.VMEM((1, 256), f32),
            pltpu.VMEM((2304, 256), bf16),
            pltpu.SemaphoreType.DMA((6,)),
            pltpu.SemaphoreType.DMA,
            pltpu.SemaphoreType.DMA,
            pltpu.SemaphoreType.DMA((6,)),
        ),
        out_specs=(
            pl.BlockSpec(memory_space=pltpu.HBM),
            pl.BlockSpec(memory_space=pltpu.VMEM),
            pl.BlockSpec(memory_space=pltpu.VMEM),
        ),
    )
    fresh = ()
    for step in range(DECODE_STEPS):
        partial = exchange(partial, NEAR)
        if step == 0:
            partial, wanted, info, cosines, sines = lax.optimization_barrier(
                (partial, wanted, info, cosines, sines)
            )
            other = lax.ppermute(wanted, "z_low", [(0, 1), (1, 0)])
        partial = call(pass_sum_kernel, shape_of((far, 8, 256)), "sum_near", (partial,))
        partial = exchange(partial, FAR)
        partial = call(pass_sum_kernel, shape_of((near, 8, 256)), "sum_far", (partial,))
        partial = exchange(partial, NEAR)
        if step == 0:
            w_out = call(
                decode_out_kernel,
                shape_of((512, 1024), bf16),
                "decode_out",
                (out_codes, out_scale.reshape(1, -1), other),
                (info,),
            )
            partial, w_out = lax.optimization_barrier((partial, w_out))
        part, new_key, new_value = call(
            functools.partial(attend_kernel, features, step),
            (shape_of((near, 8, 640)), shape_of((8, 128)), shape_of((8, 128))),
            "attend",
            (partial, cosines[step], sines[step], keys, values, *fresh),
            (info,),
            scratch=(pltpu.VMEM((64, 128), f32),),
        )
        fresh += (new_key, new_value)
        part = exchange(part, NEAR)
        part = call(pass_merge_kernel, shape_of((far, 8, 640)), "merge_near", (part,))
        part = exchange(part, FAR)
        update = call(
            finish_kernel,
            shape_of((2 * heads, 8, 128)),
            "finish",
            (part, w_out),
            (info,),
            scratch=(pltpu.VMEM((64, 128), f32),),
        )
        update = exchange(update, ("z_low", "head"))
        if step + 1 < DECODE_STEPS:
            hidden, partial = call(
                next_kernel,
                (shape_of((8, 256)), shape_of((near, 8, 256))),
                "next_step",
                (update, hidden, gain, w_qkv),
            )
    return call(last_kernel, shape_of((4, 256), bf16), "last", (update, hidden))


def solution(mesh):
    seq, head = mesh.shape["seq"], mesh.shape["head"]
    far = seq // 8
    split = Mesh(mesh.devices.reshape(far, 2, 4, head), (*SEQ, "head"))
    placed = (
        P(None, SEQ),
        P(SEQ),
        P(SEQ, "head"),
        P("head"),
        P(SEQ, "head"),
        P(SEQ),
        P(None, SEQ, "head", None),
        P(None, SEQ, "head", None),
        P(),
    )

    def run(hidden_in, *others):
        features = hidden_in.shape[1]
        return jax.shard_map(
            functools.partial(shards, float(features)),
            mesh=split,
            in_specs=placed,
            out_specs=P(None, SEQ),
            check_vma=False,
        )(hidden_in, *others)

    return run
```

```python
import functools
import math

import jax
import jax.numpy as jnp
from jax import lax
from jax.experimental import pallas as pl
from jax.experimental.pallas import tpu as pltpu
from jax.sharding import Mesh
from jax.sharding import PartitionSpec as P

HEAD_DIM = 128
GROUPS = 16
DECODE_STEPS = 2
NEAR = ("z_low", "y")
FAR = "z_high"
SEQ = (FAR, *NEAR)

CODE_NORM = 147.8
EPSILON = 1e-05
ROPE_BASE = 500000.0
SCORE_SCALE = HEAD_DIM ** (-0.5)

f32 = jnp.float32
bf16 = jnp.bfloat16
NT = (((1,), (1,)), ((), ()))


def iota(shape, axis):
    return lax.broadcasted_iota(jnp.int32, shape, axis)


def call(kernel, outs, name, arrays, scalars=(), remote=(), scratch=(), out_specs=None):
    specs = [pl.BlockSpec(memory_space=pltpu.SMEM) for _ in scalars]
    specs += [pl.BlockSpec(memory_space=pltpu.HBM) for _ in remote]
    specs += [pl.BlockSpec(memory_space=pltpu.VMEM) for _ in arrays]
    remote = [pltpu.with_memory_space_constraint(x, pltpu.HBM) for x in remote]
    return pl.pallas_call(
        kernel,
        out_shape=outs,
        in_specs=specs,
        out_specs=out_specs or jax.tree.map(lambda _: pl.BlockSpec(memory_space=pltpu.VMEM), outs),
        scratch_shapes=scratch,
        name=name,
        compiler_params=pltpu.CompilerParams(vmem_limit_bytes=16 * 1024 * 1024),
    )(*scalars, *remote, *arrays)


def shape_of(shape, dtype=f32):
    return jax.ShapeDtypeStruct(shape, dtype)


def byte_sum(state):
    x = state * 34038481 + 76625530
    pairs = (x & 0x00FF00FF) + ((x >> 8) & 0x00FF00FF)
    total = (pairs + (pairs >> 16)) & 0x7FF
    return (total - 510).astype(f32)


def interleave():
    row = iota((128, 128), 0)
    column = iota((128, 128), 1)
    return (column == 4 * (row & 31) + (row >> 5)).astype(f32).astype(bf16)


def exact_product(x, ones):
    rows = x.shape[0]
    high = x.astype(bf16).astype(f32)
    rest = x - high
    middle = rest.astype(bf16).astype(f32)
    low = rest - middle
    parts = jnp.concatenate([high, middle, low], axis=0).astype(bf16)
    product = jnp.dot(parts, ones, preferred_element_type=f32)
    return product[:rows] + product[rows : 2 * rows] + product[2 * rows :]


def tile_of(x, k):
    return x[:, k * 128 : k * 128 + 128]


def send_halves(out_ref, halves):
    copies = out_ref.shape[0] // 2
    for s in range(2):
        for j in range(copies):
            for k in range(5):
                out_ref[s * copies + j, :, k * 128 : k * 128 + 128] = halves[s][k]


def project(hidden, gain, weights, out_ref):
    squares = jnp.sum(hidden * hidden, axis=1, keepdims=True)
    normed = (hidden * gain).astype(bf16)
    y = lax.dot_general(normed, weights, NT, preferred_element_type=f32)
    first = iota((8, 128), 0) < 4
    few = iota((8, 128), 1) < 16
    spread = jnp.broadcast_to(squares, (8, 128))
    tails = [tile_of(y, 16 + k) for k in range(2)]
    tails = [jnp.where(first, tail, pltpu.roll(tail, 112, 1)) for tail in tails]
    for p in range(8):
        tail = tails[p // 4]
        if p % 4:
            tail = pltpu.roll(tail, 128 - 32 * (p % 4), 1)
        out_ref[p, :, :128] = jnp.where(first, tile_of(y, 2 * p), tile_of(y, 2 * p + 1))
        out_ref[p, :, 128:] = jnp.where(few, tail, spread)


def decode_qkv_kernel(codes_hbm, scale_hbm, gain_hbm, hidden_ref, w_ref, hid_ref, out_ref,
                      codes_ref, scale_ref, gain_ref, code_sems, scale_sem, gain_sem):
    chunks = code_sems.shape[0]
    chunk_rows = codes_ref.shape[0] // chunks
    copies = []
    for i in range(chunks):
        rows = pl.ds(i * chunk_rows, chunk_rows)
        copies.append(
            pltpu.make_async_copy(codes_hbm.at[rows], codes_ref.at[rows], code_sems.at[i])
        )
    scale_copy = pltpu.make_async_copy(scale_hbm, scale_ref, scale_sem)
    gain_copy = pltpu.make_async_copy(gain_hbm, gain_ref, gain_sem)
    scale_copy.start()
    gain_copy.start()
    for copy in copies:
        copy.start()
    scale_copy.wait()
    lane = iota((32, 128), 1)
    word = iota((32, 128), 0)
    for tile in range(18):
        if tile * 32 % chunk_rows == 0:
            copies[tile * 32 // chunk_rows].wait()
        codes = codes_ref[tile * 32 : tile * 32 + 32, :]
        window = (codes << 16) | (pltpu.roll(codes, 31, 0) << 8) | pltpu.roll(codes, 30, 0)
        scales = jnp.broadcast_to(scale_ref[tile : tile + 1, :], (32, 128)) * (1.0 / CODE_NORM)
        for r in range(4):
            column = jnp.sum(
                jnp.where(lane == 4 * word + r, scales, 0.0), axis=1, keepdims=True
            )
            values = byte_sum((window >> (8 - 2 * r)) & 0xFFFF) * column
            at = tile * 128 + r * 32
            w_ref[at : at + 32, :] = values.astype(bf16)
    hidden = hidden_ref[...].astype(f32)
    hidden = jnp.concatenate([hidden, hidden], axis=0)
    hid_ref[...] = hidden
    gain_copy.wait()
    project(hidden, gain_ref[...], w_ref[...], out_ref)


def keep_kernel(w_ref, kept_ref, sem):
    copy = pltpu.make_async_copy(w_ref, kept_ref, sem)
    copy.start()
    copy.wait()


def decode_out_kernel(info_ref, codes_ref, scale_ref, other_ref, w_ref):
    s = info_ref[5]
    lane = iota((32, 128), 1)
    within = lane & 31
    for block in range(16):
        own = block < 8
        rows = slice(block % 8 * 32, block % 8 * 32 + 32)
        across = iota((32, 256), 1) == iota((32, 256), 0) + block % 8 * 32
        scale = scale_ref[...] if own else other_ref[256:257, :]
        scale = jnp.broadcast_to(scale, (32, 256)) * (1.0 / CODE_NORM)
        column = jnp.sum(jnp.where(across, scale, 0.0), axis=1, keepdims=True)
        for group in range(2):
            if own:
                codes = jnp.where(
                    s == 0,
                    codes_ref[rows, group * 128 : group * 128 + 128],
                    codes_ref[rows, group * 128 + 256 : group * 128 + 384],
                )
            else:
                codes = other_ref[rows, group * 128 : group * 128 + 128].astype(jnp.int32)
            second = jnp.where(within < 31, pltpu.roll(codes, 127, 1), pltpu.roll(codes, 31, 1))
            third = jnp.where(within < 30, pltpu.roll(codes, 126, 1), pltpu.roll(codes, 30, 1))
            window = (codes << 16) | (second << 8) | third
            for r in range(4):
                values = byte_sum((window >> (8 - 2 * r)) & 0xFFFF) * column
                at = group * 512 + r * 128
                w_ref[block * 32 : block * 32 + 32, at : at + 128] = values.astype(bf16)


def total_of(ref):
    total = ref[0]
    for j in range(1, ref.shape[0]):
        total = total + ref[j]
    return total


def pass_sum_kernel(in_ref, out_ref):
    total = total_of(in_ref)
    for j in range(out_ref.shape[0]):
        out_ref[j] = total


def merged(in_ref):
    parts = range(in_ref.shape[0])
    stats = [in_ref[j, :, 512:] for j in parts]
    top = functools.reduce(jnp.maximum, stats)
    factors = [jnp.exp(x - top) for x in stats]
    sums = stats[0] * pltpu.roll(factors[0], 4, 1)
    for j in parts[1:]:
        sums = sums + stats[j] * pltpu.roll(factors[j], 4, 1)
    accs = []
    for b in range(4):
        at = slice(b * 128, b * 128 + 128)
        acc = in_ref[0, :, at] * factors[0][:, b : b + 1]
        for j in parts[1:]:
            acc = acc + in_ref[j, :, at] * factors[j][:, b : b + 1]
        accs.append(acc)
    return top, sums, accs


def pass_merge_kernel(in_ref, out_ref):
    top, sums, accs = merged(in_ref)
    lane = iota((8, 128), 1)
    stats = jnp.where(lane < 4, top, jnp.where(lane < 8, sums, 0.0))
    for j in range(out_ref.shape[0]):
        for b in range(4):
            out_ref[j, :, b * 128 : b * 128 + 128] = accs[b]
        out_ref[j, :, 512:] = stats


def attend_kernel(features, earlier, info_ref, in_ref, cos_ref, sin_ref, keys_ref, values_ref,
                  *refs):
    out_ref, k_ref, v_ref, q_ref = refs[2 * earlier :]
    first = iota((8, 128), 0) < 4
    lane = iota((8, 128), 1)
    rms = lax.rsqrt(in_ref[0, :, 144:145] / features + EPSILON)
    tiles = [in_ref[p, :, :128] for p in range(8)]
    for k in range(2):
        tail = in_ref[4 * k, :, 128:]
        for p in range(1, 4):
            part = pltpu.roll(in_ref[4 * k + p, :, 128:], 32 * p, 1)
            tail = jnp.where(lane >> 5 == p, part, tail)
        tail = jnp.where(first, tail, pltpu.roll(tail, 16, 1))
        tiles.append(jnp.where(lane & 31 < 16, tail, pltpu.roll(tail, 4, 0)))
    tiles = [tile * rms for tile in tiles]
    x = exact_product(jnp.concatenate(tiles, axis=0), interleave())
    cos = jnp.concatenate([cos_ref[...]] * 18, axis=0)
    sin = jnp.concatenate([sin_ref[...]] * 18, axis=0)
    turned = x[:72] * cos + pltpu.roll(x[:72], 64, 1) * sin
    turned = turned.astype(bf16).astype(f32)
    q_ref[...] = turned[:64]
    new_key = turned[64:]
    new_value = x[72:].astype(bf16).astype(f32)
    k_ref[...] = new_key
    v_ref[...] = new_value
    new_keys = [refs[2 * u][...] for u in range(earlier)] + [new_key]
    new_values = [refs[2 * u + 1][...] for u in range(earlier)] + [new_value]
    owner = info_ref[4] == 0

    def by_head(rows):
        return jnp.concatenate(
            [jnp.broadcast_to(rows[b : b + 1, :], (16, 128)) for b in range(4)], axis=0
        )

    by_sequence = [q_ref[pl.ds(b, 16, stride=4), :] for b in range(4)]
    queries = jnp.concatenate(by_sequence, axis=0)
    fresh = [
        jnp.where(
            owner,
            jnp.sum(queries * by_head(key), axis=1, keepdims=True) * SCORE_SCALE,
            -1e30,
        )
        for key in new_keys
    ]
    length = keys_ref.shape[1]
    place = iota((16, length), 1)
    halves = [[], []]
    stats = [jnp.zeros((8, 128), f32)] * 2
    tops, totals, pair_accs = [], [], []
    for pair in (0, 2):
        empty = jnp.zeros((16, 128), f32)
        both = jnp.concatenate(
            [
                jnp.concatenate([by_sequence[pair], empty], axis=1),
                jnp.concatenate([empty, by_sequence[pair + 1]], axis=1),
            ],
            axis=0,
        ).astype(bf16)
        keys = jnp.concatenate([keys_ref[pair], keys_ref[pair + 1]], axis=1)
        values = jnp.concatenate([values_ref[pair], values_ref[pair + 1]], axis=1)
        scores = lax.dot_general(both, keys, NT, preferred_element_type=f32) * SCORE_SCALE
        rounded = []
        for k in range(2):
            score = scores[16 * k : 16 * k + 16]
            live = place < info_ref[pair + k]
            top = jnp.max(jnp.where(live, score, -1e30), axis=1, keepdims=True)
            weights = jnp.where(live, jnp.exp(score - top), 0.0)
            tops.append(top)
            totals.append(jnp.sum(weights, axis=1, keepdims=True))
            rounded.append(weights.astype(bf16))
        acc = jnp.dot(
            jnp.concatenate(rounded, axis=0), values, preferred_element_type=f32
        )
        pair_accs += [acc[:16, :128], acc[16:, 128:]]
    top = jnp.concatenate(tops, axis=0)
    peak = functools.reduce(jnp.maximum, fresh, top)
    factor = jnp.exp(top - peak)
    total = jnp.concatenate(totals, axis=0) * factor
    acc = jnp.concatenate(pair_accs, axis=0) * factor
    for score, value in zip(fresh, new_values):
        weight = jnp.where(owner, jnp.exp(score - peak), 0.0)
        total = total + weight
        acc = acc + weight * by_head(value)
    for b in range(4):
        for s in range(2):
            at = b * 16 + 8 * s
            rows = slice(at, at + 8)
            halves[s].append(acc[rows])
            stats[s] = jnp.where(lane == b, peak[rows], stats[s])
            stats[s] = jnp.where(lane == 4 + b, total[rows], stats[s])
    send_halves(out_ref, [halves[s] + [stats[s]] for s in range(2)])


def finish_kernel(info_ref, in_ref, w_ref, out_ref, rows_ref):
    _, sums, accs = merged(in_ref)
    for b in range(4):
        attended = (accs[b] / sums[:, 4 + b : 5 + b]).astype(bf16).astype(f32)
        rows_ref[b * 8 : b * 8 + 8, :] = attended
        rows_ref[b * 8 + 32 : b * 8 + 40, :] = attended
    attended = jnp.concatenate(
        [rows_ref[pl.ds(t, 8, stride=8), :] for t in range(8)], axis=0
    ).astype(bf16)
    attended = lax.dot_general(attended, interleave(), NT, preferred_element_type=f32)
    block = iota((8, 128), 1) >> 5
    chunks = []
    for group in range(2):
        for r in range(4):
            chunk = jnp.zeros((8, 128), f32)
            for t in range(4):
                at = (group * 4 + t) * 8
                part = attended[at : at + 8]
                if t != r:
                    part = pltpu.roll(part, (t - r) % 4 * 32, 1)
                chunk = jnp.where(block == t, part, chunk)
            chunks.append(chunk)
    columns = jnp.concatenate(chunks, axis=1).astype(bf16)
    update = lax.dot_general(columns, w_ref[...], NT, preferred_element_type=f32)
    first = iota((8, 128), 0) < 4
    own = jnp.where(first, tile_of(update, 0), tile_of(update, 1))
    other = jnp.where(first, tile_of(update, 2), tile_of(update, 3))
    same = info_ref[5] == 0
    blocks = [jnp.where(same, own, other), jnp.where(same, other, own)]
    copies = out_ref.shape[0] // 2
    for s in range(2):
        for j in range(copies):
            out_ref[s * copies + j] = blocks[s]


def updated(in_ref, hid_ref):
    update = total_of(in_ref)
    turned = pltpu.roll(update, 4, 0)
    first = iota((8, 128), 0) < 4
    update = jnp.concatenate(
        [jnp.where(first, update, turned), jnp.where(first, turned, update)], axis=1
    )
    return (hid_ref[...] + update).astype(bf16)


def next_kernel(in_ref, hid_ref, gain_ref, w_ref, new_ref, out_ref):
    hidden = updated(in_ref, hid_ref).astype(f32)
    new_ref[...] = hidden
    project(hidden, gain_ref[...], w_ref[...], out_ref)


def last_kernel(in_ref, hid_ref, out_ref):
    out_ref[...] = updated(in_ref, hid_ref)[:4]


def exchange(value, axes):
    return lax.all_to_all(value, axes, split_axis=0, concat_axis=0, tiled=True)


def shards(features, hidden_in, norm_gain, qkv_codes, qkv_scale, out_codes, out_scale,
           cache_keys, cache_values, lengths):
    near = lax.axis_size(NEAR)
    far = lax.axis_size(FAR)
    heads = lax.axis_size("head")
    gain = norm_gain.reshape(1, -1)
    batch, block_len = cache_keys.shape[:2]
    keys = cache_keys.reshape(batch, block_len, HEAD_DIM)
    values = cache_values.reshape(batch, block_len, HEAD_DIM)
    place = lax.axis_index(SEQ)
    low = lax.axis_index("z_low")
    info = jnp.concatenate(
        [lengths - place * block_len, jnp.stack([place, low]).astype(jnp.int32)]
    )
    wanted = lax.dynamic_slice_in_dim(out_codes, (1 - low) * 256, 256, axis=1)
    wanted = jnp.concatenate(
        [wanted.astype(f32), jnp.broadcast_to(out_scale[None, :], (8, 256))], axis=0
    )

    half_dim = HEAD_DIM // 2
    freqs = jnp.exp(
        -(jnp.arange(half_dim, dtype=f32) * (2.0 / HEAD_DIM)) * math.log(ROPE_BASE)
    )
    steps = jnp.arange(DECODE_STEPS, dtype=jnp.int32)
    positions = lengths[None, :] + steps[:, None]
    angles = positions.astype(f32)[:, :, None] * freqs
    cosines, sines = jnp.cos(angles), jnp.sin(angles)
    cosines = jnp.concatenate([cosines, cosines], axis=-1)
    sines = jnp.concatenate([-sines, sines], axis=-1)
    cosines = tuple(cosines[step] for step in range(DECODE_STEPS))
    sines = tuple(sines[step] for step in range(DECODE_STEPS))

    w_qkv, hidden, partial = call(
        decode_qkv_kernel,
        (shape_of((2304, 256), bf16), shape_of((8, 256)), shape_of((near, 8, 256))),
        "decode_qkv",
        (hidden_in,),
        remote=(qkv_codes.T, qkv_scale.reshape(18, 128), gain),
        scratch=(
            pltpu.VMEM((576, 256), jnp.int32),
            pltpu.VMEM((18, 128), f32),
            pltpu.VMEM((1, 256), f32),
            pltpu.SemaphoreType.DMA((6,)),
            pltpu.SemaphoreType.DMA,
            pltpu.SemaphoreType.DMA,
        ),
    )
    w_qkv = call(
        keep_kernel,
        pltpu.HBM((2304, 256), bf16),
        "keep",
        (w_qkv,),
        scratch=(pltpu.SemaphoreType.DMA,),
        out_specs=pl.BlockSpec(memory_space=pltpu.HBM),
    )
    fresh = ()
    for step in range(DECODE_STEPS):
        partial = exchange(partial, NEAR)
        if step == 0:
            partial, w_qkv, wanted, info, cosines, sines = lax.optimization_barrier(
                (partial, w_qkv, wanted, info, cosines, sines)
            )
            other = lax.ppermute(wanted, "z_low", [(0, 1), (1, 0)])
        partial = call(pass_sum_kernel, shape_of((far, 8, 256)), "sum_near", (partial,))
        partial = exchange(partial, FAR)
        partial = call(pass_sum_kernel, shape_of((near, 8, 256)), "sum_far", (partial,))
        partial = exchange(partial, NEAR)
        if step == 0:
            w_out = call(
                decode_out_kernel,
                shape_of((512, 1024), bf16),
                "decode_out",
                (out_codes, out_scale.reshape(1, -1), other),
                (info,),
            )
            partial, w_out = lax.optimization_barrier((partial, w_out))
        part, new_key, new_value = call(
            functools.partial(attend_kernel, features, step),
            (shape_of((near, 8, 640)), shape_of((8, 128)), shape_of((8, 128))),
            "attend",
            (partial, cosines[step], sines[step], keys, values, *fresh),
            (info,),
            scratch=(pltpu.VMEM((64, 128), f32),),
        )
        fresh += (new_key, new_value)
        part = exchange(part, NEAR)
        part = call(pass_merge_kernel, shape_of((far, 8, 640)), "merge_near", (part,))
        part = exchange(part, FAR)
        update = call(
            finish_kernel,
            shape_of((2 * heads, 8, 128)),
            "finish",
            (part, w_out),
            (info,),
            scratch=(pltpu.VMEM((64, 128), f32),),
        )
        update = exchange(update, ("z_low", "head"))
        if step + 1 < DECODE_STEPS:
            hidden, partial = call(
                next_kernel,
                (shape_of((8, 256)), shape_of((near, 8, 256))),
                "next_step",
                (update, hidden, gain, w_qkv),
            )
    return call(last_kernel, shape_of((4, 256), bf16), "last", (update, hidden))


def solution(mesh):
    seq, head = mesh.shape["seq"], mesh.shape["head"]
    far = seq // 8
    split = Mesh(mesh.devices.reshape(far, 2, 4, head), (*SEQ, "head"))
    placed = (
        P(None, SEQ),
        P(SEQ),
        P(SEQ, "head"),
        P("head"),
        P(SEQ, "head"),
        P(SEQ),
        P(None, SEQ, "head", None),
        P(None, SEQ, "head", None),
        P(),
    )

    def run(hidden_in, *others):
        features = hidden_in.shape[1]
        return jax.shard_map(
            functools.partial(shards, float(features)),
            mesh=split,
            in_specs=placed,
            out_specs=P(None, SEQ),
            check_vma=False,
        )(hidden_in, *others)

    return run
```

```python
import functools
import math

import jax
import jax.numpy as jnp
from jax import lax
from jax.experimental import pallas as pl
from jax.experimental.pallas import tpu as pltpu
from jax.sharding import Mesh
from jax.sharding import PartitionSpec as P

HEAD_DIM = 128
GROUPS = 16
DECODE_STEPS = 2
NEAR = ("z_low", "y")
FAR = "z_high"
SEQ = (FAR, *NEAR)

CODE_NORM = 147.8
EPSILON = 1e-05
ROPE_BASE = 500000.0
SCORE_SCALE = HEAD_DIM ** (-0.5)

f32 = jnp.float32
bf16 = jnp.bfloat16
NT = (((1,), (1,)), ((), ()))


def iota(shape, axis):
    return lax.broadcasted_iota(jnp.int32, shape, axis)


def call(kernel, outs, name, arrays, scalars=(), remote=(), scratch=(), out_specs=None):
    specs = [pl.BlockSpec(memory_space=pltpu.SMEM) for _ in scalars]
    specs += [pl.BlockSpec(memory_space=pltpu.HBM) for _ in remote]
    specs += [pl.BlockSpec(memory_space=pltpu.VMEM) for _ in arrays]
    remote = [pltpu.with_memory_space_constraint(x, pltpu.HBM) for x in remote]
    return pl.pallas_call(
        kernel,
        out_shape=outs,
        in_specs=specs,
        out_specs=out_specs or jax.tree.map(lambda _: pl.BlockSpec(memory_space=pltpu.VMEM), outs),
        scratch_shapes=scratch,
        name=name,
        compiler_params=pltpu.CompilerParams(vmem_limit_bytes=16 * 1024 * 1024),
    )(*scalars, *remote, *arrays)


def shape_of(shape, dtype=f32):
    return jax.ShapeDtypeStruct(shape, dtype)


def byte_sum(state):
    x = state * 34038481 + 76625530
    pairs = (x & 0x00FF00FF) + ((x >> 8) & 0x00FF00FF)
    total = (pairs * 0x10001) >> 16
    return (total - 510).astype(f32)


def interleave():
    row = iota((128, 128), 0)
    column = iota((128, 128), 1)
    return (column == 4 * (row & 31) + (row >> 5)).astype(f32).astype(bf16)


def exact_product(x, ones):
    rows = x.shape[0]
    high = x.astype(bf16).astype(f32)
    rest = x - high
    middle = rest.astype(bf16).astype(f32)
    low = rest - middle
    parts = jnp.concatenate([high, middle, low], axis=0).astype(bf16)
    product = jnp.dot(parts, ones, preferred_element_type=f32)
    return product[:rows] + product[rows : 2 * rows] + product[2 * rows :]


def tile_of(x, k):
    return x[:, k * 128 : k * 128 + 128]


def send_halves(out_ref, halves):
    copies = out_ref.shape[0] // 2
    for s in range(2):
        for j in range(copies):
            for k in range(5):
                out_ref[s * copies + j, :, k * 128 : k * 128 + 128] = halves[s][k]


def project(hidden, gain, weights, out_ref):
    squares = jnp.sum(hidden * hidden, axis=1, keepdims=True)
    normed = (hidden * gain).astype(bf16)
    y = lax.dot_general(normed, weights, NT, preferred_element_type=f32)
    first = iota((8, 128), 0) < 4
    few = iota((8, 128), 1) < 16
    spread = jnp.broadcast_to(squares, (8, 128))
    tails = [tile_of(y, 16 + k) for k in range(2)]
    tails = [jnp.where(first, tail, pltpu.roll(tail, 112, 1)) for tail in tails]
    for p in range(8):
        tail = tails[p // 4]
        if p % 4:
            tail = pltpu.roll(tail, 128 - 32 * (p % 4), 1)
        out_ref[p, :, :128] = jnp.where(first, tile_of(y, 2 * p), tile_of(y, 2 * p + 1))
        out_ref[p, :, 128:] = jnp.where(few, tail, spread)


def decode_qkv_kernel(codes_hbm, scale_hbm, gain_hbm, hidden_ref, w_ref, hid_ref, out_ref,
                      codes_ref, scale_ref, gain_ref, code_sems, scale_sem, gain_sem):
    chunks = code_sems.shape[0]
    chunk_rows = codes_ref.shape[0] // chunks
    copies = []
    for i in range(chunks):
        rows = pl.ds(i * chunk_rows, chunk_rows)
        copies.append(
            pltpu.make_async_copy(codes_hbm.at[rows], codes_ref.at[rows], code_sems.at[i])
        )
    scale_copy = pltpu.make_async_copy(scale_hbm, scale_ref, scale_sem)
    gain_copy = pltpu.make_async_copy(gain_hbm, gain_ref, gain_sem)
    copies[0].start()
    scale_copy.start()
    for copy in copies[1:]:
        copy.start()
    gain_copy.start()
    scale_copy.wait()
    lane = iota((32, 128), 1)
    word = iota((32, 128), 0)
    for tile in range(18):
        if tile * 32 % chunk_rows == 0:
            copies[tile * 32 // chunk_rows].wait()
        codes = codes_ref[tile * 32 : tile * 32 + 32, :]
        window = (codes << 16) | (pltpu.roll(codes, 31, 0) << 8) | pltpu.roll(codes, 30, 0)
        scales = jnp.broadcast_to(scale_ref[tile : tile + 1, :], (32, 128)) * (1.0 / CODE_NORM)
        for r in range(4):
            column = jnp.sum(
                jnp.where(lane == 4 * word + r, scales, 0.0), axis=1, keepdims=True
            )
            values = byte_sum((window >> (8 - 2 * r)) & 0xFFFF) * column
            at = tile * 128 + r * 32
            w_ref[at : at + 32, :] = values.astype(bf16)
    hidden = hidden_ref[...].astype(f32)
    hidden = jnp.concatenate([hidden, hidden], axis=0)
    hid_ref[...] = hidden
    gain_copy.wait()
    project(hidden, gain_ref[...], w_ref[...], out_ref)


def keep_kernel(w_ref, kept_ref, sem):
    copy = pltpu.make_async_copy(w_ref, kept_ref, sem)
    copy.start()
    copy.wait()


def decode_out_kernel(info_ref, codes_ref, scale_ref, other_ref, w_ref):
    s = info_ref[5]
    lane = iota((32, 128), 1)
    within = lane & 31
    for block in range(16):
        own = block < 8
        rows = slice(block % 8 * 32, block % 8 * 32 + 32)
        across = iota((32, 256), 1) == iota((32, 256), 0) + block % 8 * 32
        scale = scale_ref[...] if own else other_ref[256:257, :]
        scale = jnp.broadcast_to(scale, (32, 256)) * (1.0 / CODE_NORM)
        column = jnp.sum(jnp.where(across, scale, 0.0), axis=1, keepdims=True)
        for group in range(2):
            if own:
                codes = jnp.where(
                    s == 0,
                    codes_ref[rows, group * 128 : group * 128 + 128],
                    codes_ref[rows, group * 128 + 256 : group * 128 + 384],
                )
            else:
                codes = other_ref[rows, group * 128 : group * 128 + 128].astype(jnp.int32)
            second = jnp.where(within < 31, pltpu.roll(codes, 127, 1), pltpu.roll(codes, 31, 1))
            third = jnp.where(within < 30, pltpu.roll(codes, 126, 1), pltpu.roll(codes, 30, 1))
            window = (codes << 16) | (second << 8) | third
            for r in range(4):
                values = byte_sum((window >> (8 - 2 * r)) & 0xFFFF) * column
                at = group * 512 + r * 128
                w_ref[block * 32 : block * 32 + 32, at : at + 128] = values.astype(bf16)


def total_of(ref):
    total = ref[0]
    for j in range(1, ref.shape[0]):
        total = total + ref[j]
    return total


def pass_sum_kernel(in_ref, out_ref):
    total = total_of(in_ref)
    for j in range(out_ref.shape[0]):
        out_ref[j] = total


def merged(in_ref):
    parts = range(in_ref.shape[0])
    stats = [in_ref[j, :, 512:] for j in parts]
    top = functools.reduce(jnp.maximum, stats)
    factors = [jnp.exp(x - top) for x in stats]
    sums = stats[0] * pltpu.roll(factors[0], 4, 1)
    for j in parts[1:]:
        sums = sums + stats[j] * pltpu.roll(factors[j], 4, 1)
    accs = []
    for b in range(4):
        at = slice(b * 128, b * 128 + 128)
        acc = in_ref[0, :, at] * factors[0][:, b : b + 1]
        for j in parts[1:]:
            acc = acc + in_ref[j, :, at] * factors[j][:, b : b + 1]
        accs.append(acc)
    return top, sums, accs


def pass_merge_kernel(in_ref, out_ref):
    top, sums, accs = merged(in_ref)
    lane = iota((8, 128), 1)
    stats = jnp.where(lane < 4, top, jnp.where(lane < 8, sums, 0.0))
    for j in range(out_ref.shape[0]):
        for b in range(4):
            out_ref[j, :, b * 128 : b * 128 + 128] = accs[b]
        out_ref[j, :, 512:] = stats


def attend_kernel(features, earlier, last_step, info_ref, in_ref, cos_ref, sin_ref, keys_ref, values_ref,
                  *refs):
    out_ref, *kept_refs, q_ref = refs[2 * earlier :]
    first = iota((8, 128), 0) < 4
    lane = iota((8, 128), 1)
    rms = lax.rsqrt(in_ref[0, :, 144:145] / features + EPSILON)
    tiles = [in_ref[p, :, :128] for p in range(8)]
    for k in range(2):
        tail = in_ref[4 * k, :, 128:]
        for p in range(1, 4):
            part = pltpu.roll(in_ref[4 * k + p, :, 128:], 32 * p, 1)
            tail = jnp.where(lane >> 5 == p, part, tail)
        tail = jnp.where(first, tail, pltpu.roll(tail, 16, 1))
        tiles.append(jnp.where(lane & 31 < 16, tail, pltpu.roll(tail, 4, 0)))
    tiles = [tile * rms for tile in tiles]
    x = exact_product(jnp.concatenate(tiles, axis=0), interleave())
    cos = jnp.concatenate([cos_ref[...]] * 18, axis=0)
    sin = jnp.concatenate([sin_ref[...]] * 18, axis=0)
    turned = x[:72] * cos + pltpu.roll(x[:72], 64, 1) * sin
    turned = turned.astype(bf16).astype(f32)
    q_ref[...] = turned[:64]
    new_key = turned[64:]
    new_value = x[72:].astype(bf16).astype(f32)
    if not last_step:
        kept_refs[0][...] = new_key
        kept_refs[1][...] = new_value
    new_keys = [refs[2 * u][...] for u in range(earlier)] + [new_key]
    new_values = [refs[2 * u + 1][...] for u in range(earlier)] + [new_value]
    owner = info_ref[4] == 0

    def by_head(rows):
        return jnp.concatenate(
            [jnp.broadcast_to(rows[b : b + 1, :], (16, 128)) for b in range(4)], axis=0
        )

    by_sequence = [q_ref[pl.ds(b, 16, stride=4), :] for b in range(4)]
    queries = jnp.concatenate(by_sequence, axis=0)
    fresh = [
        jnp.where(
            owner,
            jnp.sum(queries * by_head(key), axis=1, keepdims=True) * SCORE_SCALE,
            -1e30,
        )
        for key in new_keys
    ]
    length = keys_ref.shape[1]
    place = iota((16, length), 1)
    halves = [[], []]
    stats = [jnp.zeros((8, 128), f32)] * 2
    tops, totals, pair_accs = [], [], []
    for pair in (0, 2):
        empty = jnp.zeros((16, 128), f32)
        both = jnp.concatenate(
            [
                jnp.concatenate([by_sequence[pair], empty], axis=1),
                jnp.concatenate([empty, by_sequence[pair + 1]], axis=1),
            ],
            axis=0,
        ).astype(bf16)
        keys = jnp.concatenate([keys_ref[pair], keys_ref[pair + 1]], axis=1)
        values = jnp.concatenate([values_ref[pair], values_ref[pair + 1]], axis=1)
        scores = lax.dot_general(both, keys, NT, preferred_element_type=f32) * SCORE_SCALE
        rounded = []
        for k in range(2):
            score = scores[16 * k : 16 * k + 16]
            live = place < info_ref[pair + k]
            top = jnp.max(jnp.where(live, score, -1e30), axis=1, keepdims=True)
            weights = jnp.where(live, jnp.exp(score - top), 0.0)
            tops.append(top)
            totals.append(jnp.sum(weights, axis=1, keepdims=True))
            rounded.append(weights.astype(bf16))
        acc = jnp.dot(
            jnp.concatenate(rounded, axis=0), values, preferred_element_type=f32
        )
        pair_accs += [acc[:16, :128], acc[16:, 128:]]
    top = jnp.concatenate(tops, axis=0)
    peak = functools.reduce(jnp.maximum, fresh, top)
    factor = jnp.exp(top - peak)
    total = jnp.concatenate(totals, axis=0) * factor
    acc = jnp.concatenate(pair_accs, axis=0) * factor
    for score, value in zip(fresh, new_values):
        weight = jnp.where(owner, jnp.exp(score - peak), 0.0)
        total = total + weight
        acc = acc + weight * by_head(value)
    for b in range(4):
        for s in range(2):
            at = b * 16 + 8 * s
            rows = slice(at, at + 8)
            halves[s].append(acc[rows])
            stats[s] = jnp.where(lane == b, peak[rows], stats[s])
            stats[s] = jnp.where(lane == 4 + b, total[rows], stats[s])
    send_halves(out_ref, [halves[s] + [stats[s]] for s in range(2)])


def finish_kernel(info_ref, in_ref, w_ref, out_ref, rows_ref):
    _, sums, accs = merged(in_ref)
    for b in range(4):
        attended = (accs[b] / sums[:, 4 + b : 5 + b]).astype(bf16).astype(f32)
        rows_ref[b * 8 : b * 8 + 8, :] = attended
        rows_ref[b * 8 + 32 : b * 8 + 40, :] = attended
    attended = jnp.concatenate(
        [rows_ref[pl.ds(t, 8, stride=8), :] for t in range(8)], axis=0
    ).astype(bf16)
    attended = lax.dot_general(attended, interleave(), NT, preferred_element_type=f32)
    block = iota((8, 128), 1) >> 5
    chunks = []
    for group in range(2):
        for r in range(4):
            chunk = jnp.zeros((8, 128), f32)
            for t in range(4):
                at = (group * 4 + t) * 8
                part = attended[at : at + 8]
                if t != r:
                    part = pltpu.roll(part, (t - r) % 4 * 32, 1)
                chunk = jnp.where(block == t, part, chunk)
            chunks.append(chunk)
    columns = jnp.concatenate(chunks, axis=1).astype(bf16)
    update = lax.dot_general(columns, w_ref[...], NT, preferred_element_type=f32)
    first = iota((8, 128), 0) < 4
    own = jnp.where(first, tile_of(update, 0), tile_of(update, 1))
    other = jnp.where(first, tile_of(update, 2), tile_of(update, 3))
    same = info_ref[5] == 0
    blocks = [jnp.where(same, own, other), jnp.where(same, other, own)]
    copies = out_ref.shape[0] // 2
    for s in range(2):
        for j in range(copies):
            out_ref[s * copies + j] = blocks[s]


def updated(in_ref, hid_ref):
    update = total_of(in_ref)
    turned = pltpu.roll(update, 4, 0)
    first = iota((8, 128), 0) < 4
    update = jnp.concatenate(
        [jnp.where(first, update, turned), jnp.where(first, turned, update)], axis=1
    )
    return (hid_ref[...] + update).astype(bf16)


def next_kernel(in_ref, hid_ref, gain_ref, w_ref, new_ref, out_ref):
    hidden = updated(in_ref, hid_ref).astype(f32)
    new_ref[...] = hidden
    project(hidden, gain_ref[...], w_ref[...], out_ref)


def last_kernel(in_ref, hid_ref, out_ref):
    out_ref[...] = updated(in_ref, hid_ref)[:4]


def exchange(value, axes):
    return lax.all_to_all(value, axes, split_axis=0, concat_axis=0, tiled=True)


def shards(features, hidden_in, norm_gain, qkv_codes, qkv_scale, out_codes, out_scale,
           cache_keys, cache_values, lengths):
    near = lax.axis_size(NEAR)
    far = lax.axis_size(FAR)
    heads = lax.axis_size("head")
    gain = norm_gain.reshape(1, -1)
    batch, block_len = cache_keys.shape[:2]
    keys = cache_keys.reshape(batch, block_len, HEAD_DIM)
    values = cache_values.reshape(batch, block_len, HEAD_DIM)
    place = lax.axis_index(SEQ)
    low = lax.axis_index("z_low")
    info = jnp.concatenate(
        [lengths - place * block_len, jnp.stack([place, low]).astype(jnp.int32)]
    )
    wanted = lax.dynamic_slice_in_dim(out_codes, (1 - low) * 256, 256, axis=1)
    wanted = jnp.concatenate(
        [wanted.astype(f32), jnp.broadcast_to(out_scale[None, :], (8, 256))], axis=0
    )

    half_dim = HEAD_DIM // 2
    freqs = jnp.exp(
        -(jnp.arange(half_dim, dtype=f32) * (2.0 / HEAD_DIM)) * math.log(ROPE_BASE)
    )
    steps = jnp.arange(DECODE_STEPS, dtype=jnp.int32)
    positions = lengths[None, :] + steps[:, None]
    angles = positions.astype(f32)[:, :, None] * freqs
    cosines, sines = jnp.cos(angles), jnp.sin(angles)
    cosines = jnp.concatenate([cosines, cosines], axis=-1)
    sines = jnp.concatenate([-sines, sines], axis=-1)
    cosines = tuple(cosines[step] for step in range(DECODE_STEPS))
    sines = tuple(sines[step] for step in range(DECODE_STEPS))

    w_qkv, hidden, partial = call(
        decode_qkv_kernel,
        (shape_of((2304, 256), bf16), shape_of((8, 256)), shape_of((near, 8, 256))),
        "decode_qkv",
        (hidden_in,),
        remote=(qkv_codes.T, qkv_scale.reshape(18, 128), gain),
        scratch=(
            pltpu.VMEM((576, 256), jnp.int32),
            pltpu.VMEM((18, 128), f32),
            pltpu.VMEM((1, 256), f32),
            pltpu.SemaphoreType.DMA((6,)),
            pltpu.SemaphoreType.DMA,
            pltpu.SemaphoreType.DMA,
        ),
    )
    w_qkv = call(
        keep_kernel,
        pltpu.HBM((2304, 256), bf16),
        "keep",
        (w_qkv,),
        scratch=(pltpu.SemaphoreType.DMA,),
        out_specs=pl.BlockSpec(memory_space=pltpu.HBM),
    )
    fresh = ()
    for step in range(DECODE_STEPS):
        partial = exchange(partial, NEAR)
        if step == 0:
            partial, w_qkv, wanted, info, cosines, sines = lax.optimization_barrier(
                (partial, w_qkv, wanted, info, cosines, sines)
            )
            other = lax.ppermute(wanted, "z_low", [(0, 1), (1, 0)])
        partial = call(pass_sum_kernel, shape_of((far, 8, 256)), "sum_near", (partial,))
        partial = exchange(partial, FAR)
        partial = call(pass_sum_kernel, shape_of((near, 8, 256)), "sum_far", (partial,))
        partial = exchange(partial, NEAR)
        if step == 0:
            w_out = call(
                decode_out_kernel,
                shape_of((512, 1024), bf16),
                "decode_out",
                (out_codes, out_scale.reshape(1, -1), other),
                (info,),
            )
            partial, w_out = lax.optimization_barrier((partial, w_out))
        last_step = step + 1 == DECODE_STEPS
        kept = () if last_step else (shape_of((8, 128)), shape_of((8, 128)))
        part, *new = call(
            functools.partial(attend_kernel, features, step, last_step),
            (shape_of((near, 8, 640)), *kept),
            "attend",
            (partial, cosines[step], sines[step], keys, values, *fresh),
            (info,),
            scratch=(pltpu.VMEM((64, 128), f32),),
        )
        fresh += tuple(new)
        part = exchange(part, NEAR)
        part = call(pass_merge_kernel, shape_of((far, 8, 640)), "merge_near", (part,))
        part = exchange(part, FAR)
        update = call(
            finish_kernel,
            shape_of((2 * heads, 8, 128)),
            "finish",
            (part, w_out),
            (info,),
            scratch=(pltpu.VMEM((64, 128), f32),),
        )
        update = exchange(update, ("z_low", "head"))
        if not last_step:
            hidden, partial = call(
                next_kernel,
                (shape_of((8, 256)), shape_of((near, 8, 256))),
                "next_step",
                (update, hidden, gain, w_qkv),
            )
    return call(last_kernel, shape_of((4, 256), bf16), "last", (update, hidden))


def solution(mesh):
    seq, head = mesh.shape["seq"], mesh.shape["head"]
    far = seq // 8
    split = Mesh(mesh.devices.reshape(far, 2, 4, head), (*SEQ, "head"))
    placed = (
        P(None, SEQ),
        P(SEQ),
        P(SEQ, "head"),
        P("head"),
        P(SEQ, "head"),
        P(SEQ),
        P(None, SEQ, "head", None),
        P(None, SEQ, "head", None),
        P(),
    )

    def run(hidden_in, *others):
        features = hidden_in.shape[1]
        return jax.shard_map(
            functools.partial(shards, float(features)),
            mesh=split,
            in_specs=placed,
            out_specs=P(None, SEQ),
            check_vma=False,
        )(hidden_in, *others)

    return run
```
